32 devices in a mesh: ctx: 8 (over z, x), tp: 4 (over y, core).
Axes of the slice: x: 2, y: 2, z: 4, core: 2. Of those that a mesh axis runs over, the one named last changes fastest.
Arguments:
- projections: bfloat16 [2048, 3, 8192], P('ctx', None, 'tp'), may hold values from -6 to 6
- short_filter: float32 [3, 3, 8192], P(None, None, 'tp'), may hold values from -3 to 3
- decay_rates: float32 [16, 8192], P(None, 'tp'), may hold values from 1.4648437e-05 to 1
- residues: float32 [16, 8192], P(None, 'tp'), may hold values from -2.4 to 2.4
- out_weight: bfloat16 [8192, 4096], P('tp'), may hold values from -0.0625 to 0.0625
Outputs:
- projected: bfloat16 [2048, 4096], P(('ctx', 'tp'))
The draws below stay inside these ranges and needn't reach their ends.
All inputs are finite; a program needn't handle non-finite values.
Results may differ from the reference program's by a relative error of at most 0.005.
Values may be sent and summed in bfloat16 or wider, within the bound.
A program may use at most 320 MiB of HBM per device.

```python
import math
import jax
import jax.numpy as jnp
from jax import lax

D = 8192
DOUT = 4096
MODES = 16
STRETCH = 64
TOKENS = 2048
N_TP = 4


def draw_decay_rates(key, part):
    base = jax.random.fold_in(key, 7001)
    key_slow, key_fast, key_pick = jax.random.split(base, 3)
    fast_share = 0.0625
    fast_low = 0.08
    fast_high = 0.6
    slow_low = math.log(0.03 / TOKENS)
    slow_high = math.log(0.03)
    slow = jnp.exp(jax.random.uniform(key_slow, (MODES, D), jnp.float32, slow_low, slow_high))
    fast = jnp.exp(jax.random.uniform(key_fast, (MODES, D), jnp.float32, math.log(fast_low), math.log(fast_high)))
    picked = jax.random.uniform(key_pick, (MODES, D), jnp.float32) < fast_share
    return jnp.where(picked, fast, slow).astype(jnp.float32)


def block_scale(rng, shape, cuts, smallest, high):
    def one(dim, shards_of):
        draws = jax.random.uniform(jax.random.fold_in(jax.random.fold_in(rng, 6), dim), (shards_of,), jnp.float32, smallest / len(cuts), high / len(cuts))
        return jnp.repeat(jnp.exp(draws), shape[dim] // shards_of).reshape((-1,) + (1,) * (len(shape) - dim - 1))

    factor_of = one(*cuts[0])
    for cut in cuts[1:]:
        factor_of = factor_of * one(*cut)
    return factor_of


def normal_values(key, extent, scale, limit, cuts=(), kind=jnp.bfloat16):
    values = jax.random.normal(key, extent, jnp.float32) * scale
    if len(cuts) > 0:
        values = block_scale(key, extent, cuts, -0.22, 0.18) * values
    return jnp.clip(values, min=-limit, max=limit).astype(kind)


def setup_inputs(seed: int = 0) -> dict:
    streams_of = jax.random.split(jax.random.key(seed), 6)
    projections = normal_values(streams_of[0], (TOKENS, 3, D), 1.0, 6.0, ((0, 8), (2, 4)))
    short_filter = normal_values(streams_of[1], (3, 3, D), 0.6, 3.0, ((2, 4),), jnp.float32)
    decay_rates = draw_decay_rates(jax.random.fold_in(streams_of[5], 71), 0)
    residues = normal_values(streams_of[3], (MODES, D), 0.4, 2.4, ((1, 4),), jnp.float32)
    out_weight = normal_values(streams_of[4], (D, DOUT), D ** -0.5, 0.0625, ((0, 4),))
    return {"projections": projections, "short_filter": short_filter, "decay_rates": decay_rates, "residues": residues, "out_weight": out_weight}


def make_tables(rates, weights_in, block_len):
    scaled = weights_in * jnp.sqrt(2.0 * rates)
    offsets = jnp.arange(block_len).astype(jnp.float32)
    hvalues = lax.optimization_barrier(jnp.sum(scaled[None] * jnp.exp(-rates[None] * offsets[:, None, None]), axis=1))
    spread = (jnp.arange(block_len)[:, None] - jnp.arange(block_len)[None, :]).astype(jnp.int32)
    toeplitz = jnp.where((spread >= 0)[:, :, None], hvalues[jnp.clip(spread, 0, block_len - 1)], 0.0)
    ending = jnp.exp(-rates[None] * (block_len - 1.0 - offsets)[:, None, None])
    entering = scaled[None] * jnp.exp(-rates[None] * (offsets + 1.0)[:, None, None])
    return (toeplitz, ending, entering)

def causal_conv(product, rates, weights_in):
    tok_rows, channels = product.shape
    blocks_count = tok_rows // STRETCH
    toeplitz, ending, entering = make_tables(rates, weights_in, STRETCH)
    pieces = product.reshape(blocks_count, STRETCH, channels)
    hp = lax.Precision.HIGHEST
    inner = jnp.einsum('tsc,ksc->ktc', toeplitz, pieces, precision=hp)
    ends = jnp.einsum('snc,ksc->knc', ending, pieces, precision=hp)
    step_decay = jnp.exp(-rates * STRETCH)

    def advance(state, end_block):
        return (step_decay * state + end_block, state)
    _, states_in = lax.scan(advance, jnp.zeros(rates.shape, jnp.float32), ends)
    outer = jnp.einsum('tnc,knc->ktc', entering, states_in, precision=hp)
    return (inner + outer).reshape(tok_rows, channels)

def reference(projections, short_filter, decay_rates, residues, out_weight):
    group_width = D // N_TP

    def one_group(group_index):
        start = group_index * group_width
        feats = lax.dynamic_slice_in_dim(projections, start, group_width, 2).astype(jnp.float32)
        taps = lax.dynamic_slice_in_dim(short_filter, start, group_width, 2)
        rates = lax.dynamic_slice_in_dim(decay_rates, start, group_width, 1)
        weights_in = lax.dynamic_slice_in_dim(residues, start, group_width, 1)
        padded = jnp.pad(feats, ((2, 0), (0, 0), (0, 0)))
        featured = taps[0] * padded[2:] + taps[1] * padded[1:-1] + taps[2] * padded[:-2]
        product = featured[:, 1, :] * featured[:, 2, :]
        convolved = causal_conv(product, rates, weights_in)
        return (featured[:, 0, :] * convolved).astype(jnp.bfloat16)
    groups = lax.map(one_group, jnp.arange(N_TP, dtype=jnp.int32))
    gated = jnp.transpose(groups, (1, 0, 2)).reshape(TOKENS, D)
    return jnp.dot(gated, out_weight, preferred_element_type=jnp.float32).astype(jnp.bfloat16)
```

```python
import functools

import jax
import jax.numpy as jnp
from jax import lax
from jax.experimental import pallas as pl
from jax.experimental.pallas import tpu as pltpu
from jax.sharding import PartitionSpec as P

LANES = 128
CHUNKS = 8
GROUPS = 4
HALO_GROUP = 2
MXU = 256
WIDTH = 512
TAIL = 16
MESH = pl.DeviceIdType.MESH
F32 = jnp.float32
BF16 = jnp.bfloat16


def summed(terms):
    while terms.shape[0] % 2 == 0:
        middle = terms.shape[0] // 2
        terms = terms[:middle] + terms[middle:]
    return jnp.sum(terms, axis=0)


def kernel(
    n_ctx, x_hbm, taps_hbm, rates_hbm, res_hbm, w_hbm, out_ref,
    xb, tails, taps_ref, rates_ref, res_ref, order, back, xs, pf, qf, yl, gp, ga, gb, wv, pt, raw, base, fades, hb,
    halo_out, halo_in, st_out, twin_in, both_out, st_in,
    own_end, decay_all, carry, first, keep, kept, pair_out, pair_in, own_out, own_in, far_out, far_in,
    x_sem, in_sem, w_sem, halo_sem, twin_send, twin_recv, st_send, st_recv,
    pair_send, pair_recv, own_send, own_recv, far_send, far_recv,
):
    me = lax.axis_index("ctx")
    tp = lax.axis_index("tp")
    pair, odd = me // 2, me % 2
    twin = pair * 2 + (1 - odd)
    chip, core = tp // 2, tp % 2
    sibling = chip * 2 + (1 - core)
    opposite = (1 - chip) * 2 + core
    toks, channels = xb.shape[1], xb.shape[2]
    modes = rates_ref.shape[0]
    half = toks // 2
    step = half // CHUNKS
    rows = half + 2 * CHUNKS
    tiles = channels // LANES
    per_group = tiles // GROUPS
    gwidth = channels // GROUPS
    blocks = gwidth // MXU
    per_block = MXU // LANES
    n_out = w_hbm.shape[1] // WIDTH
    share = toks // 4
    early = 1 - chip

    def group(g):
        return pl.ds(g * gwidth, gwidth)

    def x_copy(g):
        return pltpu.make_async_copy(
            x_hbm.at[1:3, :, group(g)], xb.at[1:3, :, group(g)], x_sem.at[g]
        )

    tail_copy = pltpu.make_async_copy(x_hbm.at[:, toks - TAIL :, :], tails, in_sem.at[0])
    rates_copy = pltpu.make_async_copy(rates_hbm, rates_ref, in_sem.at[1])
    taps_copy = pltpu.make_async_copy(taps_hbm, taps_ref, in_sem.at[2])
    res_copy = pltpu.make_async_copy(res_hbm, res_ref, in_sem.at[3])
    gate_copy = pltpu.make_async_copy(x_hbm.at[0], xb.at[0], in_sem.at[4])
    w_copy = pltpu.make_async_copy(w_hbm, wv, w_sem)

    rates_copy.start()
    taps_copy.start()
    x_copy(0).start()
    res_copy.start()
    tail_copy.start()
    for g in range(1, GROUPS):
        x_copy(g).start()
    gate_copy.start()
    w_copy.start()

    barrier = pltpu.get_barrier_semaphore()

    @pl.loop(1, n_ctx)
    def _(k):
        pl.semaphore_signal(
            barrier, inc=1, device_id=(lax.rem(me + k, n_ctx), tp), device_id_type=MESH
        )

    for other in (sibling, opposite):
        pl.semaphore_signal(barrier, inc=1, device_id=(me, other), device_id_type=MESH)

    for b in range(2):
        row = lax.broadcasted_iota(jnp.int32, (rows, toks), 0)
        token = lax.broadcasted_iota(jnp.int32, (rows, toks), 1)
        start = early * half if b == 0 else chip * half
        wanted = start + (row % CHUNKS) * step + row // CHUNKS - 2
        order[b * rows : (b + 1) * rows, :] = jnp.where(token == wanted, 1.0, 0.0).astype(BF16)
    token = lax.broadcasted_iota(jnp.int32, (half, half), 0)
    row = lax.broadcasted_iota(jnp.int32, (half, half), 1)
    back[...] = jnp.where(token == (row % CHUNKS) * step + row // CHUNKS, 1.0, 0.0).astype(BF16)

    place = lax.broadcasted_iota(jnp.int32, (1, CHUNKS, LANES), 1)
    spots = place.astype(F32) * float(step)
    to_end = float((CHUNKS - 1) * step) - spots
    late_block = jnp.where(chip == 0, 1.0, 0.0).astype(F32)

    def spread(values):
        return jnp.broadcast_to(values[:, None, :], (values.shape[0], CHUNKS, LANES))

    def lanes(c):
        return pl.ds(pl.multiple_of(c * LANES, LANES), LANES)

    def reorder(j, k):
        cols = pl.ds(pl.multiple_of(k * MXU, MXU), MXU)
        moved = jnp.dot(order[...], xb[j, :, cols], preferred_element_type=F32)
        for b in range(2):
            for t in range(per_block):
                xs[j, b, k * per_block + t] = moved[b * rows : (b + 1) * rows, t * LANES : (t + 1) * LANES]

    def feature(j, b, c, low, high):
        lane = lanes(c)
        total = None
        for i in range(3):
            at = (2 - i) * CHUNKS
            term = taps_ref[i, j : j + 1, lane] * xs[j, b, c, at + low : at + high, :]
            total = term if total is None else total + term
        return total

    def ends(c):
        decay = spread(jnp.exp(-rates_ref[:, lanes(c)]))
        for b in range(2):
            product = feature(1, b, c, 0, half) * feature(2, b, c, 0, half)
            pf[b, c] = product
            state = jnp.broadcast_to(product[None, :CHUNKS], (modes, CHUNKS, LANES))
            for i in range(1, step):
                state = decay * state + product[None, i * CHUNKS : (i + 1) * CHUNKS]
            raw[b, c] = state

    def finish(c):
        lane = lanes(c)
        rates = rates_ref[:, lane]
        decay = spread(jnp.exp(-rates))
        two = 2 * CHUNKS
        for j in (1, 2):
            xs[j, early, c, 0:1, :] = halo_in[2 * j : 2 * j + 1, lane]
            xs[j, early, c, CHUNKS : CHUNKS + 1, :] = halo_in[2 * j + 1 : 2 * j + 2, lane]
        product = feature(1, early, c, 0, two) * feature(2, early, c, 0, two)
        change = product - pf[early, c, :two, :]
        pf[early, c, :two, :] = product
        grown = decay * change[None, :CHUNKS] + change[None, CHUNKS:]
        raw[early, c] = raw[early, c] + spread(jnp.exp(-rates * float(step - 2))) * grown
        whole = jnp.exp(-rates * float(half))
        mixed = spread(whole) * raw[early, c] + raw[chip, c]
        end = jnp.sum(jnp.exp(-spread(rates) * to_end) * mixed, axis=1)
        own_end[:, lane] = end
        st_out[:, lane] = end.astype(BF16)
        decay_all[:, lane] = jnp.exp(-rates * float(toks))

    def scanned(state, rates):
        for reach in (1, 2, 4):
            fade = spread(jnp.exp(-rates * float(step * reach)))
            moved = pltpu.roll(state, reach, 1)
            state = state + jnp.where(place >= reach, fade * moved, 0.0)
        return jnp.where(place >= 1, pltpu.roll(state, 1, 1), 0.0), state[:, CHUNKS - 1, :]

    def near(b, c):
        for i in range(step):
            total = None
            for k in range(i + 1):
                at = (i - k) * CHUNKS
                term = hb[c, k] * pf[b, c, at : at + CHUNKS, :]
                total = term if total is None else total + term
            yl[c, i * CHUNKS : (i + 1) * CHUNKS, :] = total

    def responses(c):
        lane = lanes(c)
        rates = rates_ref[:, lane]
        decay = jnp.exp(-rates)
        now = res_ref[:, lane] * jnp.sqrt(2.0 * rates)
        for i in range(step):
            hb[c, i] = jnp.broadcast_to(jnp.sum(now, axis=0, keepdims=True), (CHUNKS, LANES))
            now = now * decay

    def gates(b, c):
        lane = lanes(c)
        if b == 0:
            xs[0, early, c, 0:1, :] = halo_in[0:1, lane]
            xs[0, early, c, CHUNKS : CHUNKS + 1, :] = halo_in[1:2, lane]
        qf[c] = feature(0, b, c, 0, half)

    def weights(lane, rates):
        return res_ref[:, lane] * jnp.sqrt(2.0 * rates) * jnp.exp(-rates)

    def ahead(c):
        lane = lanes(c)
        rates = rates_ref[:, lane]
        before, total = scanned(raw[0, c], rates)
        other = jnp.sum(jnp.exp(-spread(rates) * to_end) * raw[1, c], axis=1)
        first[:, lane] = jnp.where(chip == 0, other, total)
        weight = spread(weights(lane, rates))
        into = jnp.exp(-spread(rates) * spots)
        fades[c] = weight * into * spread(jnp.exp(-rates * (float(half) * late_block)))
        base[c] = weight * (before + into * spread(other * late_block))
        gates(0, c)
        near(0, c)

    def emit(c, state):
        lane = lanes(c)
        decay = spread(jnp.exp(-rates_ref[:, lane]))
        for i in range(0, step, 2):
            parts = []
            for k in (i, i + 1):
                at = slice(k * CHUNKS, (k + 1) * CHUNKS)
                parts.append(qf[c, at, :] * (yl[c, at, :] + summed(state)))
                state = decay * state
            gp[i * CHUNKS : (i + 2) * CHUNKS, lane] = jnp.concatenate(parts, axis=0).astype(BF16)

    def carried_tile(c):
        emit(c, base[c] + fades[c] * spread(carry[:, lanes(c)]))

    def own_tile(c):
        lane = lanes(c)
        rates = rates_ref[:, lane]
        before, _ = scanned(raw[1, c], rates)
        into = carry[:, lane]
        into = jnp.where(chip == 1, jnp.exp(-rates * float(half)) * into + first[:, lane], into)
        state = spread(weights(lane, rates)) * (before + jnp.exp(-spread(rates) * spots) * spread(into))
        gates(1, c)
        near(1, c)
        emit(c, state)

    def restore(into, k):
        cols = pl.ds(pl.multiple_of(k * MXU, MXU), MXU)
        into[:, cols] = jnp.dot(back[...], gp[:, cols], preferred_element_type=F32).astype(BF16)

    halo_copy = pltpu.make_async_remote_copy(
        src_ref=halo_out, dst_ref=halo_in, send_sem=halo_sem.at[0], recv_sem=halo_sem.at[1],
        device_id=(lax.rem(me + 1, n_ctx), tp), device_id_type=MESH,
    )

    def twin_copy(g):
        return pltpu.make_async_remote_copy(
            src_ref=st_out.at[:, group(g)], dst_ref=twin_in.at[:, group(g)],
            send_sem=twin_send.at[g], recv_sem=twin_recv.at[g],
            device_id=(twin, tp), device_id_type=MESH,
        )

    def state_copy(g, src, dst):
        return pltpu.make_async_remote_copy(
            src_ref=both_out.at[:, group(g)], dst_ref=st_in.at[src, :, group(g)],
            send_sem=st_send.at[dst, g], recv_sem=st_recv.at[src, g],
            device_id=(dst * 2 + odd, tp), device_id_type=MESH,
        )

    def send_both(g):
        cols = group(g)
        twin_copy(g).wait_recv()
        other = twin_in[:, cols].astype(F32)
        own = own_end[:, cols]
        fade = decay_all[:, cols]
        total = jnp.where(odd == 1, fade * other + own, fade * own + other)
        both_out[:, cols] = total.astype(BF16)

        @pl.loop(pair + 1, n_ctx // 2)
        def _(dst):
            state_copy(g, pair, dst).start()

    def group_ends(g):
        x_copy(g).wait()

        @pl.loop(g * blocks, (g + 1) * blocks)
        def _(k):
            for j in (1, 2):
                reorder(j, k)

            @pl.loop(k * per_block, (k + 1) * per_block)
            def _(c):
                ends(c)

    def group_finish(g):
        @pl.loop(g * per_group, (g + 1) * per_group)
        def _(c):
            finish(c)

        twin_copy(g).start()

    tail_copy.wait()
    for j in range(3):
        halo_out[2 * j : 2 * j + 2, :] = tails[j].astype(F32)[TAIL - 2 :]
    halo_out[6:8, :] = jnp.zeros((2, channels), F32)
    rates_copy.wait()
    taps_copy.wait()
    group_ends(0)

    pl.semaphore_wait(barrier, n_ctx + 1)

    @pl.when(me < n_ctx - 1)
    def _():
        halo_copy.start()

    for g in range(1, GROUPS):
        group_ends(g)
        if g == HALO_GROUP:
            @pl.when(me == 0)
            def _():
                halo_in[...] = jnp.zeros_like(halo_in)

            @pl.when(me > 0)
            def _():
                halo_copy.wait_recv()

            for before in range(g):
                group_finish(before)
        if g >= HALO_GROUP:
            group_finish(g)

    res_copy.wait()
    gate_copy.wait()

    for g in range(GROUPS):
        @pl.loop(g * blocks, (g + 1) * blocks)
        def _(k):
            reorder(0, k)

            @pl.loop(k * per_block, (k + 1) * per_block)
            def _(c):
                responses(c)
                ahead(c)

        if g == GROUPS - 2:
            for sent in range(g + 1):
                send_both(sent)
    send_both(GROUPS - 1)

    for g in range(GROUPS):
        cols = group(g)
        carry[:, cols] = jnp.zeros((modes, gwidth), F32)

        @pl.loop(0, pair)
        def _(src):
            fade = decay_all[:, cols] * decay_all[:, cols]
            state_copy(g, src, pair).wait_recv()
            carry[:, cols] = fade * carry[:, cols] + st_in[src, :, cols].astype(F32)

        @pl.when(odd == 1)
        def _():
            carry[:, cols] = decay_all[:, cols] * carry[:, cols] + twin_in[:, cols].astype(F32)

        @pl.loop(g * blocks, (g + 1) * blocks)
        def _(k):
            @pl.loop(k * per_block, (k + 1) * per_block)
            def _(c):
                carried_tile(c)

            restore(ga, k)

    w_copy.wait()

    def to_sibling(n, out, into, send, recv):
        return pltpu.make_async_remote_copy(
            src_ref=out.at[n], dst_ref=into.at[n], send_sem=send.at[n], recv_sem=recv.at[n],
            device_id=(me, sibling), device_id_type=MESH,
        )

    def pair_copy(n):
        return to_sibling(n, pair_out, pair_in, pair_send, pair_recv)

    def own_copy(n):
        return to_sibling(n, own_out, own_in, own_send, own_recv)

    def far_copy(n):
        return pltpu.make_async_remote_copy(
            src_ref=far_out.at[n], dst_ref=far_in.at[n],
            send_sem=far_send.at[n], recv_sem=far_recv.at[n],
            device_id=(me, opposite), device_id_type=MESH,
        )

    mine = pl.ds(pl.multiple_of(core * share, share), share)
    theirs = pl.ds(pl.multiple_of((1 - core) * share, share), share)

    def forward(n):
        pair_copy(n).wait_recv()
        far_out[n] = (keep[n] + pair_in[n].astype(F32)).astype(BF16)
        far_copy(n).start()

    def columns(n):
        return pl.ds(pl.multiple_of(n * WIDTH, WIDTH), WIDTH)

    @pl.loop(0, n_out)
    def _(n):
        pt[...] = jnp.dot(ga[...], wv[:, columns(n)], preferred_element_type=F32)
        pair_out[n] = pt[theirs, :].astype(BF16)
        pair_copy(n).start()
        keep[n] = pt[mine, :]

        @pl.when(n > 0)
        def _():
            forward(n - 1)

    forward(n_out - 1)

    @pl.loop(0, channels // MXU)
    def _(k):
        @pl.loop(k * per_block, (k + 1) * per_block)
        def _(c):
            own_tile(c)

        restore(gb, k)

    @pl.loop(0, n_out)
    def _(n):
        pt[...] = jnp.dot(gb[...], wv[:, columns(n)], preferred_element_type=F32)
        own_out[n] = pt[theirs, :].astype(BF16)
        own_copy(n).start()
        kept[n] = pt[mine, :]

    @pl.loop(0, n_out)
    def _(n):
        own_copy(n).wait_recv()
        far_copy(n).wait_recv()
        total = kept[n] + own_in[n].astype(F32) + far_in[n].astype(F32)
        out_ref[:, columns(n)] = total.astype(BF16)

    @pl.loop(0, n_out)
    def _(n):
        pair_copy(n).wait_send()
        own_copy(n).wait_send()
        far_copy(n).wait_send()

    for g in range(GROUPS):
        twin_copy(g).wait_send()

        @pl.loop(pair + 1, n_ctx // 2)
        def _(dst):
            state_copy(g, pair, dst).wait_send()

    @pl.when(me < n_ctx - 1)
    def _():
        halo_copy.wait_send()


def per_device(n_ctx, projections, short_filter, decay_rates, residues, out_weight):
    x = jnp.transpose(projections, (1, 0, 2))
    _, toks, channels = x.shape
    modes = decay_rates.shape[0]
    dout = out_weight.shape[1]
    tiles = channels // LANES
    n_out = dout // WIDTH
    share = toks // 4
    half = toks // 2
    step = half // CHUNKS
    rows = half + 2 * CHUNKS
    dma = pltpu.SemaphoreType.DMA
    hbm = pl.BlockSpec(memory_space=pltpu.HBM)
    operands = [
        pltpu.with_memory_space_constraint(a, pltpu.HBM)
        for a in (x, short_filter, decay_rates, residues, out_weight)
    ]
    return pl.pallas_call(
        functools.partial(kernel, n_ctx),
        out_shape=jax.ShapeDtypeStruct((share, dout), BF16),
        in_specs=[hbm] * 5,
        out_specs=pl.BlockSpec(memory_space=pltpu.VMEM),
        scratch_shapes=[
            pltpu.VMEM((3, toks, channels), BF16),
            pltpu.VMEM((3, TAIL, channels), BF16),
            pltpu.VMEM(short_filter.shape, F32),
            pltpu.VMEM((modes, channels), F32),
            pltpu.VMEM((modes, channels), F32),
            pltpu.VMEM((2 * rows, toks), BF16),
            pltpu.VMEM((half, half), BF16),
            pltpu.VMEM((3, 2, tiles, rows, LANES), F32),
            pltpu.VMEM((2, tiles, half, LANES), F32),
            pltpu.VMEM((tiles, half, LANES), F32),
            pltpu.VMEM((tiles, half, LANES), F32),
            pltpu.VMEM((half, channels), BF16),
            pltpu.VMEM((half, channels), BF16),
            pltpu.VMEM((half, channels), BF16),
            pltpu.VMEM((channels, dout), BF16),
            pltpu.VMEM((half, WIDTH), F32),
            pltpu.VMEM((2, tiles, modes, CHUNKS, LANES), F32),
            pltpu.VMEM((tiles, modes, CHUNKS, LANES), F32),
            pltpu.VMEM((tiles, modes, CHUNKS, LANES), F32),
            pltpu.VMEM((tiles, step, CHUNKS, LANES), F32),
            pltpu.VMEM((8, channels), F32),
            pltpu.VMEM((8, channels), F32),
            pltpu.VMEM((modes, channels), BF16),
            pltpu.VMEM((modes, channels), BF16),
            pltpu.VMEM((modes, channels), BF16),
            pltpu.VMEM((n_ctx // 2, modes, channels), BF16),
            pltpu.VMEM((modes, channels), F32),
            pltpu.VMEM((modes, channels), F32),
            pltpu.VMEM((modes, channels), F32),
            pltpu.VMEM((modes, channels), F32),
            pltpu.VMEM((n_out, share, WIDTH), F32),
            pltpu.VMEM((n_out, share, WIDTH), F32),
            pltpu.VMEM((n_out, share, WIDTH), BF16),
            pltpu.VMEM((n_out, share, WIDTH), BF16),
            pltpu.VMEM((n_out, share, WIDTH), BF16),
            pltpu.VMEM((n_out, share, WIDTH), BF16),
            pltpu.VMEM((n_out, share, WIDTH), BF16),
            pltpu.VMEM((n_out, share, WIDTH), BF16),
            dma((GROUPS,)), dma((5,)), dma, dma((2,)),
            dma((GROUPS,)), dma((GROUPS,)),
            dma((n_ctx // 2, GROUPS)), dma((n_ctx // 2, GROUPS)),
            dma((n_out,)), dma((n_out,)), dma((n_out,)), dma((n_out,)),
            dma((n_out,)), dma((n_out,)),
        ],
        compiler_params=pltpu.CompilerParams(
            collective_id=0, has_side_effects=True, vmem_limit_bytes=48 * 2**20
        ),
    )(*operands)


def solution(mesh):
    placed = (
        P("ctx", None, "tp"),
        P(None, None, "tp"),
        P(None, "tp"),
        P(None, "tp"),
        P("tp", None),
    )
    return jax.shard_map(
        functools.partial(per_device, mesh.shape["ctx"]),
        mesh=mesh, in_specs=placed, out_specs=P(("ctx", "tp"), None), check_vma=False,
    )
```

```python
import functools

import jax
import jax.numpy as jnp
from jax import lax
from jax.experimental import pallas as pl
from jax.experimental.pallas import tpu as pltpu
from jax.sharding import PartitionSpec as P

LANES = 128
CHUNKS = 8
UNITS = 4
HALO_GROUP = 2
MXU = 256
WIDTH = 512
TAIL = 16
MESH = pl.DeviceIdType.MESH
F32 = jnp.float32
BF16 = jnp.bfloat16


def summed(terms):
    while terms.shape[0] % 2 == 0:
        middle = terms.shape[0] // 2
        terms = terms[:middle] + terms[middle:]
    return jnp.sum(terms, axis=0)


def kernel(
    n_ctx, x_hbm, taps_hbm, rates_hbm, res_hbm, w_hbm, out_ref,
    xb, tails, taps_ref, rates_ref, res_ref, order, back, xs_even, xs_odd, pf, qf, yl, gp, ga, gb, wv, pt, raw, base, fades, hb,
    halo_out, halo_in, st_out, twin_in, both_out, st_in,
    own_end, decay_all, carry, first, keep, kept, pair_out, pair_in, own_out, own_in, far_out, far_in,
    x_sem, in_sem, w_sem, halo_sem, twin_send, twin_recv, st_send, st_recv,
    pair_send, pair_recv, own_send, own_recv, far_send, far_recv,
):
    me = lax.axis_index("ctx")
    tp = lax.axis_index("tp")
    pair, odd = me // 2, me % 2
    twin = pair * 2 + (1 - odd)
    chip, core = tp // 2, tp % 2
    sibling = chip * 2 + (1 - core)
    opposite = (1 - chip) * 2 + core
    toks, channels = xb.shape[1], xb.shape[2]
    modes = rates_ref.shape[0]
    half = toks // 2
    step = half // CHUNKS
    rows = half + 2 * CHUNKS
    gwidth = UNITS * LANES
    groups = channels // gwidth
    per_block = MXU // LANES
    n_out = w_hbm.shape[1] // WIDTH
    share = toks // 4
    early = 1 - chip

    def group(g):
        return pl.ds(pl.multiple_of(g * gwidth, gwidth), gwidth)

    def x_copy(g):
        return pltpu.make_async_copy(x_hbm.at[:, :, group(g)], xb.at[:, :, group(g)], x_sem.at[g])

    tail_copy = pltpu.make_async_copy(x_hbm.at[:, toks - TAIL :, :], tails, in_sem.at[0])
    rates_copy = pltpu.make_async_copy(rates_hbm, rates_ref, in_sem.at[1])
    taps_copy = pltpu.make_async_copy(taps_hbm, taps_ref, in_sem.at[2])
    res_copy = pltpu.make_async_copy(res_hbm, res_ref, in_sem.at[3])
    w_copy = pltpu.make_async_copy(w_hbm, wv, w_sem)

    rates_copy.start()
    taps_copy.start()
    x_copy(0).start()
    res_copy.start()
    tail_copy.start()

    @pl.loop(1, groups)
    def _(g):
        x_copy(g).start()

    w_copy.start()

    barrier = pltpu.get_barrier_semaphore()

    @pl.loop(1, n_ctx)
    def _(k):
        pl.semaphore_signal(
            barrier, inc=1, device_id=(lax.rem(me + k, n_ctx), tp), device_id_type=MESH
        )

    for other in (sibling, opposite):
        pl.semaphore_signal(barrier, inc=1, device_id=(me, other), device_id_type=MESH)

    for b in range(2):
        row = lax.broadcasted_iota(jnp.int32, (rows, toks), 0)
        token = lax.broadcasted_iota(jnp.int32, (rows, toks), 1)
        start = early * half if b == 0 else chip * half
        wanted = start + (row % CHUNKS) * step + row // CHUNKS - 2
        order[b * rows : (b + 1) * rows, :] = jnp.where(token == wanted, 1.0, 0.0).astype(BF16)
    token = lax.broadcasted_iota(jnp.int32, (half, half), 0)
    row = lax.broadcasted_iota(jnp.int32, (half, half), 1)
    back[...] = jnp.where(token == (row % CHUNKS) * step + row // CHUNKS, 1.0, 0.0).astype(BF16)

    place = lax.broadcasted_iota(jnp.int32, (1, CHUNKS, LANES), 1)
    spots = place.astype(F32) * float(step)
    to_end = float((CHUNKS - 1) * step) - spots
    late_block = jnp.where(chip == 0, 1.0, 0.0).astype(F32)

    def spread(values):
        return jnp.broadcast_to(values[:, None, :], (values.shape[0], CHUNKS, LANES))

    def lanes(c):
        return pl.ds(pl.multiple_of(c * LANES, LANES), LANES)

    def collapse(terms):
        spot = place[0]
        out = []
        for f in range(0, len(terms), CHUNKS):
            v = terms[f : f + CHUNKS]
            low = spot < 4
            y = [
                jnp.where(low, v[n], v[n + 4]) + pltpu.roll(jnp.where(low, v[n + 4], v[n]), 4, 0)
                for n in range(4)
            ]
            low = spot % 4 < 2
            z = [
                jnp.where(low, y[n] + pltpu.roll(y[n], 6, 0), y[n + 2] + pltpu.roll(y[n + 2], 2, 0))
                for n in range(2)
            ]
            low = spot % 2 == 0
            out.append(jnp.where(low, z[0] + pltpu.roll(z[0], 7, 0), z[1] + pltpu.roll(z[1], 1, 0)))
        return jnp.concatenate(out, axis=0)

    def over_chunks(terms):
        return collapse([terms[n] for n in range(modes)])

    def ordered(g, u):
        return (xs_even, xs_odd)[u // per_block], g * per_block + u % per_block

    def reorder(g, which):
        cols = pl.ds(pl.multiple_of(g * gwidth + which * MXU, MXU), MXU)
        for j in range(3):
            moved = jnp.dot(order[...], xb[j, :, cols], preferred_element_type=F32)
            for b in range(2):
                for u in range(which * per_block, (which + 1) * per_block):
                    xs, at = ordered(g, u)
                    left = u % per_block * LANES
                    xs[j, b, at] = moved[b * rows : (b + 1) * rows, left : left + LANES]

    def feature(j, b, g, u, low, high):
        lane = lanes(g * UNITS + u)
        xs, where = ordered(g, u)
        total = None
        for i in range(3):
            at = (2 - i) * CHUNKS
            term = taps_ref[i, j : j + 1, lane] * xs[j, b, where, at + low : at + high, :]
            total = term if total is None else total + term
        return total

    def add_halo(j, g, u):
        lane = lanes(g * UNITS + u)
        xs, where = ordered(g, u)
        xs[j, early, where, 0:1, :] = halo_in[2 * j : 2 * j + 1, lane]
        xs[j, early, where, CHUNKS : CHUNKS + 1, :] = halo_in[2 * j + 1 : 2 * j + 2, lane]

    def ends(g, u):
        c = g * UNITS + u
        decay = spread(jnp.exp(-rates_ref[:, lanes(c)]))
        for b in range(2):
            product = feature(1, b, g, u, 0, half) * feature(2, b, g, u, 0, half)
            pf[b, c] = product
            state = jnp.broadcast_to(product[None, :CHUNKS], (modes, CHUNKS, LANES))
            for i in range(1, step):
                state = decay * state + product[None, i * CHUNKS : (i + 1) * CHUNKS]
            raw[b, c] = state

    def finish(g, u):
        c = g * UNITS + u
        lane = lanes(c)
        rates = rates_ref[:, lane]
        decay = spread(jnp.exp(-rates))
        two = 2 * CHUNKS
        for j in (1, 2):
            add_halo(j, g, u)
        product = feature(1, early, g, u, 0, two) * feature(2, early, g, u, 0, two)
        change = product - pf[early, c, :two, :]
        pf[early, c, :two, :] = product
        grown = decay * change[None, :CHUNKS] + change[None, CHUNKS:]
        fixed = raw[early, c] + spread(jnp.exp(-rates * float(step - 2))) * grown
        raw[early, c] = fixed
        mixed = spread(jnp.exp(-rates * float(half))) * fixed + raw[chip, c]
        end = over_chunks(jnp.exp(-spread(rates) * to_end) * mixed)
        own_end[:, lane] = end
        st_out[:, lane] = end.astype(BF16)
        decay_all[:, lane] = jnp.exp(-rates * float(toks))

    def scanned(state, rates):
        for reach in (1, 2, 4):
            fade = spread(jnp.exp(-rates * float(step * reach)))
            moved = pltpu.roll(state, reach, 1)
            state = state + jnp.where(place >= reach, fade * moved, 0.0)
        return jnp.where(place >= 1, pltpu.roll(state, 1, 1), 0.0), state[:, CHUNKS - 1, :]

    def near(b, c):
        for i in range(step):
            total = None
            for k in range(i + 1):
                at = (i - k) * CHUNKS
                term = hb[c, k : k + 1, :] * pf[b, c, at : at + CHUNKS, :]
                total = term if total is None else total + term
            yl[c, i * CHUNKS : (i + 1) * CHUNKS, :] = total

    def responses(c):
        lane = lanes(c)
        rates = rates_ref[:, lane]
        decay = jnp.exp(-rates)
        now = res_ref[:, lane] * jnp.sqrt(2.0 * rates)
        terms = []
        for i in range(step):
            terms.append(summed(now.reshape(modes // CHUNKS, CHUNKS, LANES)))
            now = now * decay
        hb[c] = collapse(terms)

    def gates(b, g, u):
        if b == 0:
            add_halo(0, g, u)
        qf[g * UNITS + u] = feature(0, b, g, u, 0, half)

    def weights(lane, rates):
        return res_ref[:, lane] * jnp.sqrt(2.0 * rates) * jnp.exp(-rates)

    def ahead(g, u):
        c = g * UNITS + u
        lane = lanes(c)
        rates = rates_ref[:, lane]
        before, total = scanned(raw[0, c], rates)
        other = over_chunks(jnp.exp(-spread(rates) * to_end) * raw[1, c])
        first[:, lane] = jnp.where(chip == 0, other, total)
        weight = spread(weights(lane, rates))
        into = jnp.exp(-spread(rates) * spots)
        fades[c] = weight * into * spread(jnp.exp(-rates * (float(half) * late_block)))
        base[c] = weight * (before + into * spread(other * late_block))
        gates(0, g, u)
        near(0, c)

    def emit(c, state):
        lane = lanes(c)
        decay = spread(jnp.exp(-rates_ref[:, lane]))
        for i in range(0, step, 2):
            parts = []
            for k in (i, i + 1):
                at = slice(k * CHUNKS, (k + 1) * CHUNKS)
                parts.append(qf[c, at, :] * (yl[c, at, :] + summed(state)))
                state = decay * state
            gp[i * CHUNKS : (i + 2) * CHUNKS, lane] = jnp.concatenate(parts, axis=0).astype(BF16)

    def carried_tile(c):
        emit(c, base[c] + fades[c] * spread(carry[:, lanes(c)]))

    def own_tile(g, u):
        c = g * UNITS + u
        lane = lanes(c)
        rates = rates_ref[:, lane]
        before, _ = scanned(raw[1, c], rates)
        into = carry[:, lane]
        into = jnp.where(chip == 1, jnp.exp(-rates * float(half)) * into + first[:, lane], into)
        state = spread(weights(lane, rates)) * (before + jnp.exp(-spread(rates) * spots) * spread(into))
        gates(1, g, u)
        near(1, c)
        emit(c, state)

    def restore(into, g):
        cols = group(g)
        into[:, cols] = jnp.dot(back[...], gp[:, cols], preferred_element_type=F32).astype(BF16)

    halo_copy = pltpu.make_async_remote_copy(
        src_ref=halo_out, dst_ref=halo_in, send_sem=halo_sem.at[0], recv_sem=halo_sem.at[1],
        device_id=(lax.rem(me + 1, n_ctx), tp), device_id_type=MESH,
    )

    def twin_copy(g):
        return pltpu.make_async_remote_copy(
            src_ref=st_out.at[:, group(g)], dst_ref=twin_in.at[:, group(g)],
            send_sem=twin_send.at[g], recv_sem=twin_recv.at[g],
            device_id=(twin, tp), device_id_type=MESH,
        )

    def state_copy(g, src, dst):
        return pltpu.make_async_remote_copy(
            src_ref=both_out.at[:, group(g)], dst_ref=st_in.at[src, :, group(g)],
            send_sem=st_send.at[dst, g], recv_sem=st_recv.at[src, g],
            device_id=(dst * 2 + odd, tp), device_id_type=MESH,
        )

    def send_both(g):
        cols = group(g)
        twin_copy(g).wait_recv()
        other = twin_in[:, cols].astype(F32)
        own = own_end[:, cols]
        fade = decay_all[:, cols]
        total = jnp.where(odd == 1, fade * other + own, fade * own + other)
        both_out[:, cols] = total.astype(BF16)

        @pl.loop(pair + 1, n_ctx // 2)
        def _(dst):
            state_copy(g, pair, dst).start()

    tail_copy.wait()
    for j in range(3):
        halo_out[2 * j : 2 * j + 2, :] = tails[j].astype(F32)[TAIL - 2 :]
    halo_out[6:8, :] = jnp.zeros((2, channels), F32)
    rates_copy.wait()
    taps_copy.wait()
    x_copy(0).wait()
    reorder(0, 0)

    @pl.loop(0, groups)
    def _(g):
        @pl.when(g < groups - 1)
        def _():
            x_copy(g + 1).wait()

        reorder(g, 1)
        ends(g, 0)
        ends(g, 1)
        reorder((g + 1) % groups, 0)
        ends(g, 2)
        ends(g, 3)

        @pl.when(g == 0)
        def _():
            pl.semaphore_wait(barrier, n_ctx + 1)

            @pl.when(me < n_ctx - 1)
            def _():
                halo_copy.start()

        @pl.when(g == HALO_GROUP)
        def _():
            @pl.when(me == 0)
            def _():
                halo_in[...] = jnp.zeros_like(halo_in)

            @pl.when(me > 0)
            def _():
                halo_copy.wait_recv()

        low = jnp.where(g == HALO_GROUP, 0, g)
        high = jnp.where(g < HALO_GROUP, low, g + 1)

        @pl.loop(low, high)
        def _(k):
            for u in range(UNITS):
                finish(k, u)
            twin_copy(k).start()

    res_copy.wait()

    @pl.loop(0, groups)
    def _(g):
        for u in range(UNITS):
            responses(g * UNITS + u)
            ahead(g, u)

        @pl.when(g == groups - 2)
        def _():
            @pl.loop(0, groups)
            def _(k):
                send_both(k)

    @pl.loop(0, groups)
    def _(g):
        cols = group(g)
        carry[:, cols] = jnp.zeros((modes, gwidth), F32)

        @pl.loop(0, pair)
        def _(src):
            fade = decay_all[:, cols] * decay_all[:, cols]
            state_copy(g, src, pair).wait_recv()
            carry[:, cols] = fade * carry[:, cols] + st_in[src, :, cols].astype(F32)

        @pl.when(odd == 1)
        def _():
            carry[:, cols] = decay_all[:, cols] * carry[:, cols] + twin_in[:, cols].astype(F32)

        for u in range(UNITS):
            carried_tile(g * UNITS + u)
        restore(ga, g)

    w_copy.wait()

    def to_sibling(n, out, into, send, recv):
        return pltpu.make_async_remote_copy(
            src_ref=out.at[n], dst_ref=into.at[n], send_sem=send.at[n], recv_sem=recv.at[n],
            device_id=(me, sibling), device_id_type=MESH,
        )

    def pair_copy(n):
        return to_sibling(n, pair_out, pair_in, pair_send, pair_recv)

    def own_copy(n):
        return to_sibling(n, own_out, own_in, own_send, own_recv)

    def far_copy(n):
        return pltpu.make_async_remote_copy(
            src_ref=far_out.at[n], dst_ref=far_in.at[n],
            send_sem=far_send.at[n], recv_sem=far_recv.at[n],
            device_id=(me, opposite), device_id_type=MESH,
        )

    mine = pl.ds(pl.multiple_of(core * share, share), share)
    theirs = pl.ds(pl.multiple_of((1 - core) * share, share), share)

    def forward(n):
        pair_copy(n).wait_recv()
        far_out[n] = (keep[n] + pair_in[n].astype(F32)).astype(BF16)
        far_copy(n).start()

    def columns(n):
        return pl.ds(pl.multiple_of(n * WIDTH, WIDTH), WIDTH)

    @pl.loop(0, n_out)
    def _(n):
        pt[...] = jnp.dot(ga[...], wv[:, columns(n)], preferred_element_type=F32)
        pair_out[n] = pt[theirs, :].astype(BF16)
        pair_copy(n).start()
        keep[n] = pt[mine, :]

        @pl.when(n > 0)
        def _():
            forward(n - 1)

    forward(n_out - 1)

    @pl.loop(0, groups)
    def _(g):
        for u in range(UNITS):
            own_tile(g, u)
        restore(gb, g)

    @pl.loop(0, n_out)
    def _(n):
        pt[...] = jnp.dot(gb[...], wv[:, columns(n)], preferred_element_type=F32)
        own_out[n] = pt[theirs, :].astype(BF16)
        own_copy(n).start()
        kept[n] = pt[mine, :]

    @pl.loop(0, n_out)
    def _(n):
        own_copy(n).wait_recv()
        far_copy(n).wait_recv()
        total = kept[n] + own_in[n].astype(F32) + far_in[n].astype(F32)
        out_ref[:, columns(n)] = total.astype(BF16)

    @pl.loop(0, n_out)
    def _(n):
        pair_copy(n).wait_send()
        own_copy(n).wait_send()
        far_copy(n).wait_send()

    @pl.loop(0, groups)
    def _(g):
        twin_copy(g).wait_send()

        @pl.loop(pair + 1, n_ctx // 2)
        def _(dst):
            state_copy(g, pair, dst).wait_send()

    @pl.when(me < n_ctx - 1)
    def _():
        halo_copy.wait_send()


def per_device(n_ctx, projections, short_filter, decay_rates, residues, out_weight):
    x = jnp.transpose(projections, (1, 0, 2))
    _, toks, channels = x.shape
    modes = decay_rates.shape[0]
    dout = out_weight.shape[1]
    tiles = channels // LANES
    groups = tiles // UNITS
    n_out = dout // WIDTH
    share = toks // 4
    half = toks // 2
    step = half // CHUNKS
    rows = half + 2 * CHUNKS
    dma = pltpu.SemaphoreType.DMA
    hbm = pl.BlockSpec(memory_space=pltpu.HBM)
    operands = [
        pltpu.with_memory_space_constraint(a, pltpu.HBM)
        for a in (x, short_filter, decay_rates, residues, out_weight)
    ]
    return pl.pallas_call(
        functools.partial(kernel, n_ctx),
        out_shape=jax.ShapeDtypeStruct((share, dout), BF16),
        in_specs=[hbm] * 5,
        out_specs=pl.BlockSpec(memory_space=pltpu.VMEM),
        scratch_shapes=[
            pltpu.VMEM((3, toks, channels), BF16),
            pltpu.VMEM((3, TAIL, channels), BF16),
            pltpu.VMEM(short_filter.shape, F32),
            pltpu.VMEM((modes, channels), F32),
            pltpu.VMEM((modes, channels), F32),
            pltpu.VMEM((2 * rows, toks), BF16),
            pltpu.VMEM((half, half), BF16),
            pltpu.VMEM((3, 2, tiles // 2, rows, LANES), F32),
            pltpu.VMEM((3, 2, tiles // 2, rows, LANES), F32),
            pltpu.VMEM((2, tiles, half, LANES), F32),
            pltpu.VMEM((tiles, half, LANES), F32),
            pltpu.VMEM((tiles, half, LANES), F32),
            pltpu.VMEM((half, channels), BF16),
            pltpu.VMEM((half, channels), BF16),
            pltpu.VMEM((half, channels), BF16),
            pltpu.VMEM((channels, dout), BF16),
            pltpu.VMEM((half, WIDTH), F32),
            pltpu.VMEM((2, tiles, modes, CHUNKS, LANES), F32),
            pltpu.VMEM((tiles, modes, CHUNKS, LANES), F32),
            pltpu.VMEM((tiles, modes, CHUNKS, LANES), F32),
            pltpu.VMEM((tiles, step, LANES), F32),
            pltpu.VMEM((8, channels), F32),
            pltpu.VMEM((8, channels), F32),
            pltpu.VMEM((modes, channels), BF16),
            pltpu.VMEM((modes, channels), BF16),
            pltpu.VMEM((modes, channels), BF16),
            pltpu.VMEM((n_ctx // 2, modes, channels), BF16),
            pltpu.VMEM((modes, channels), F32),
            pltpu.VMEM((modes, channels), F32),
            pltpu.VMEM((modes, channels), F32),
            pltpu.VMEM((modes, channels), F32),
            pltpu.VMEM((n_out, share, WIDTH), F32),
            pltpu.VMEM((n_out, share, WIDTH), F32),
            pltpu.VMEM((n_out, share, WIDTH), BF16),
            pltpu.VMEM((n_out, share, WIDTH), BF16),
            pltpu.VMEM((n_out, share, WIDTH), BF16),
            pltpu.VMEM((n_out, share, WIDTH), BF16),
            pltpu.VMEM((n_out, share, WIDTH), BF16),
            pltpu.VMEM((n_out, share, WIDTH), BF16),
            dma((groups,)), dma((4,)), dma, dma((2,)),
            dma((groups,)), dma((groups,)),
            dma((n_ctx // 2, groups)), dma((n_ctx // 2, groups)),
            dma((n_out,)), dma((n_out,)), dma((n_out,)), dma((n_out,)),
            dma((n_out,)), dma((n_out,)),
        ],
        compiler_params=pltpu.CompilerParams(
            collective_id=0, has_side_effects=True, vmem_limit_bytes=48 * 2**20
        ),
    )(*operands)


def solution(mesh):
    placed = (
        P("ctx", None, "tp"),
        P(None, None, "tp"),
        P(None, "tp"),
        P(None, "tp"),
        P("tp", None),
    )
    return jax.shard_map(
        functools.partial(per_device, mesh.shape["ctx"]),
        mesh=mesh, in_specs=placed, out_specs=P(("ctx", "tp"), None), check_vma=False,
    )
```

```python
import functools

import jax
import jax.numpy as jnp
from jax import lax
from jax.experimental import pallas as pl
from jax.experimental.pallas import tpu as pltpu
from jax.sharding import PartitionSpec as P

LANES = 128
CHUNKS = 8
UNITS = 4
HALO_GROUP = 2
MXU = 256
WIDTH = 512
FIRST = (1, 0)
SECOND = (2, 1)
LAG = 2
TAIL = 16
MESH = pl.DeviceIdType.MESH
F32 = jnp.float32
BF16 = jnp.bfloat16


def summed(terms):
    while terms.shape[0] % 2 == 0:
        middle = terms.shape[0] // 2
        terms = terms[:middle] + terms[middle:]
    return jnp.sum(terms, axis=0)


def kernel(
    n_ctx, x_hbm, taps_hbm, rates_hbm, res_hbm, w_hbm, out_ref,
    xb, tails, taps_ref, rates_ref, res_ref, order, back, xs_even, xs_odd, pf, qf, yl, gp, ga, gb, wv, pt, raw, base, fades, hb,
    halo_out, halo_in, st_out, twin_in, both_out, st_in,
    own_end, decay_all, carry, first, keep, kept, pair_out, pair_in, own_out, own_in, far_out, far_in,
    x_sem, in_sem, w_sem, halo_sem, twin_send, twin_recv, st_send, st_recv,
    pair_send, pair_recv, own_send, own_recv, far_send, far_recv,
):
    me = lax.axis_index("ctx")
    tp = lax.axis_index("tp")
    pair, odd = me // 2, me % 2
    twin = pair * 2 + (1 - odd)
    chip, core = tp // 2, tp % 2
    sibling = chip * 2 + (1 - core)
    opposite = (1 - chip) * 2 + core
    toks, channels = xb.shape[1], xb.shape[2]
    modes = rates_ref.shape[0]
    half = toks // 2
    step = half // CHUNKS
    rows = half + 2 * CHUNKS
    gwidth = UNITS * LANES
    tiles = channels // LANES
    groups = channels // gwidth
    per_block = MXU // LANES
    n_out = w_hbm.shape[1] // WIDTH
    share = toks // 4
    early = 1 - chip

    def group(g):
        return pl.ds(pl.multiple_of(g * gwidth, gwidth), gwidth)

    def x_copy(g):
        return pltpu.make_async_copy(x_hbm.at[:, :, group(g)], xb.at[:, :, group(g)], x_sem.at[g])

    tail_copy = pltpu.make_async_copy(x_hbm.at[:, toks - TAIL :, :], tails, in_sem.at[0])
    rates_copy = pltpu.make_async_copy(rates_hbm, rates_ref, in_sem.at[1])
    taps_copy = pltpu.make_async_copy(taps_hbm, taps_ref, in_sem.at[2])
    res_copy = pltpu.make_async_copy(res_hbm, res_ref, in_sem.at[3])
    w_copy = pltpu.make_async_copy(w_hbm, wv, w_sem)

    rates_copy.start()
    res_copy.start()
    x_copy(0).start()
    taps_copy.start()
    tail_copy.start()

    @pl.loop(1, groups)
    def _(g):
        x_copy(g).start()

    w_copy.start()

    barrier = pltpu.get_barrier_semaphore()

    @pl.loop(1, n_ctx)
    def _(k):
        pl.semaphore_signal(
            barrier, inc=1, device_id=(lax.rem(me + k, n_ctx), tp), device_id_type=MESH
        )

    for other in (sibling, opposite):
        pl.semaphore_signal(barrier, inc=1, device_id=(me, other), device_id_type=MESH)

    for b in range(2):
        row = lax.broadcasted_iota(jnp.int32, (rows, toks), 0)
        token = lax.broadcasted_iota(jnp.int32, (rows, toks), 1)
        start = early * half if b == 0 else chip * half
        wanted = start + (row % CHUNKS) * step + row // CHUNKS - 2
        order[b * rows : (b + 1) * rows, :] = jnp.where(token == wanted, 1.0, 0.0).astype(BF16)
    token = lax.broadcasted_iota(jnp.int32, (half, half), 0)
    row = lax.broadcasted_iota(jnp.int32, (half, half), 1)
    back[...] = jnp.where(token == (row % CHUNKS) * step + row // CHUNKS, 1.0, 0.0).astype(BF16)

    place = lax.broadcasted_iota(jnp.int32, (1, CHUNKS, LANES), 1)
    spots = place.astype(F32) * float(step)
    to_end = float((CHUNKS - 1) * step) - spots
    late_block = jnp.where(chip == 0, 1.0, 0.0).astype(F32)

    def spread(values):
        return jnp.broadcast_to(values[:, None, :], (values.shape[0], CHUNKS, LANES))

    def lanes(c):
        return pl.ds(pl.multiple_of(c * LANES, LANES), LANES)

    def collapse(terms):
        spot = place[0]
        out = []
        for f in range(0, len(terms), CHUNKS):
            v = terms[f : f + CHUNKS]
            low = spot < 4
            y = [
                jnp.where(low, v[n], v[n + 4]) + pltpu.roll(jnp.where(low, v[n + 4], v[n]), 4, 0)
                for n in range(4)
            ]
            low = spot % 4 < 2
            z = [
                jnp.where(low, y[n] + pltpu.roll(y[n], 6, 0), y[n + 2] + pltpu.roll(y[n + 2], 2, 0))
                for n in range(2)
            ]
            low = spot % 2 == 0
            out.append(jnp.where(low, z[0] + pltpu.roll(z[0], 7, 0), z[1] + pltpu.roll(z[1], 1, 0)))
        return jnp.concatenate(out, axis=0)

    def over_chunks(terms):
        return collapse([terms[n] for n in range(modes)])

    def ordered(g, u):
        return (xs_even, xs_odd)[u // per_block], g * per_block + u % per_block

    def reorder(g, which):
        cols = pl.ds(pl.multiple_of(g * gwidth + which * MXU, MXU), MXU)
        for j in range(3):
            moved = jnp.dot(order[...], xb[j, :, cols], preferred_element_type=F32)
            for b in range(2):
                for u in range(which * per_block, (which + 1) * per_block):
                    xs, at = ordered(g, u)
                    left = u % per_block * LANES
                    xs[j, b, at] = moved[b * rows : (b + 1) * rows, left : left + LANES]

    def feature(j, b, g, u, low, high):
        lane = lanes(g * UNITS + u)
        xs, where = ordered(g, u)
        total = None
        for i in range(3):
            at = (2 - i) * CHUNKS
            term = taps_ref[i, j : j + 1, lane] * xs[j, b, where, at + low : at + high, :]
            total = term if total is None else total + term
        return total

    def add_halo(j, g, u):
        lane = lanes(g * UNITS + u)
        xs, where = ordered(g, u)
        xs[j, early, where, 0:1, :] = halo_in[2 * j : 2 * j + 1, lane]
        xs[j, early, where, CHUNKS : CHUNKS + 1, :] = halo_in[2 * j + 1 : 2 * j + 2, lane]

    def ends(g, u, last=None):
        c = g * UNITS + u
        lane = lanes(c)
        rates = spread(rates_ref[:, lane])
        decay = jnp.exp(-rates)
        mixed = None
        for b in range(2):
            product = feature(1, b, g, u, 0, half) * feature(2, b, g, u, 0, half)
            pf[b, c] = product
            opening = product[:CHUNKS]
            if last is not None:
                opening = opening + 0.0 * last
            state = jnp.broadcast_to(opening[None], (modes, CHUNKS, LANES))
            for i in range(1, step):
                state = decay * state + product[None, i * CHUNKS : (i + 1) * CHUNKS]
            raw[b, c] = state.reshape(modes * CHUNKS, LANES)
            last = state[modes - 1]
            after = to_end + float(half) * (1.0 - late_block if b == 0 else late_block)
            part = jnp.exp(-rates * after) * state
            mixed = part if mixed is None else mixed + part
        own_end[:, lane] = over_chunks(mixed)
        return last

    def finish(g, u):
        c = g * UNITS + u
        lane = lanes(c)
        rates = rates_ref[:, lane]
        two = 2 * CHUNKS
        for j in (1, 2):
            add_halo(j, g, u)
        product = feature(1, early, g, u, 0, two) * feature(2, early, g, u, 0, two)
        change = product - pf[early, c, :two, :]
        pf[early, c, :two, :] = product
        grown = jnp.exp(-rates) * change[:1] + change[CHUNKS : CHUNKS + 1]
        grown = jnp.exp(-rates * float(step - 2)) * grown
        heads = pl.ds(0, modes, stride=CHUNKS)
        raw[early, c, heads, :] = raw[early, c, heads, :] + grown
        end = own_end[:, lane] + jnp.exp(-rates * float(toks - step)) * grown
        own_end[:, lane] = end
        st_out[:, lane] = end.astype(BF16)

    def states_of(b, c):
        return raw[b, c].reshape(modes, CHUNKS, LANES)

    def scanned(state, rates):
        for reach in (1, 2, 4):
            fade = spread(jnp.exp(-rates * float(step * reach)))
            moved = pltpu.roll(state, reach, 1)
            state = state + jnp.where(place >= reach, fade * moved, 0.0)
        return jnp.where(place >= 1, pltpu.roll(state, 1, 1), 0.0), state[:, CHUNKS - 1, :]

    def near(b, c):
        for i in range(step):
            total = None
            for k in range(i + 1):
                at = (i - k) * CHUNKS
                term = hb[c, k : k + 1, :] * pf[b, c, at : at + CHUNKS, :]
                total = term if total is None else total + term
            yl[c, i * CHUNKS : (i + 1) * CHUNKS, :] = total

    def responses(c):
        lane = lanes(c)
        rates = rates_ref[:, lane]
        decay = jnp.exp(-rates)
        now = res_ref[:, lane] * jnp.sqrt(2.0 * rates)
        terms = []
        for i in range(step):
            terms.append(summed(now.reshape(modes // CHUNKS, CHUNKS, LANES)))
            now = now * decay
        hb[c] = collapse(terms)
        decay_all[:, lane] = jnp.exp(-rates * float(toks))

    def gates(b, g, u):
        if b == 0:
            add_halo(0, g, u)
        qf[g * UNITS + u] = feature(0, b, g, u, 0, half)

    def weights(lane, rates):
        return res_ref[:, lane] * jnp.sqrt(2.0 * rates) * jnp.exp(-rates)

    def ahead(g, u):
        c = g * UNITS + u
        lane = lanes(c)
        rates = rates_ref[:, lane]
        before, total = scanned(states_of(0, c), rates)
        other = over_chunks(jnp.exp(-spread(rates) * to_end) * states_of(1, c))
        first[:, lane] = jnp.where(chip == 0, other, total)
        weight = spread(weights(lane, rates))
        into = jnp.exp(-spread(rates) * spots)
        fades[c] = weight * into * spread(jnp.exp(-rates * (float(half) * late_block)))
        base[c] = weight * (before + into * spread(other * late_block))
        gates(0, g, u)
        near(0, c)

    def emit(c, state):
        lane = lanes(c)
        decay = spread(jnp.exp(-rates_ref[:, lane]))
        for i in range(0, step, 2):
            parts = []
            for k in (i, i + 1):
                at = slice(k * CHUNKS, (k + 1) * CHUNKS)
                parts.append(qf[c, at, :] * (yl[c, at, :] + summed(state)))
                state = decay * state
            gp[i * CHUNKS : (i + 2) * CHUNKS, lane] = jnp.concatenate(parts, axis=0).astype(BF16)

    def carried_tile(c):
        emit(c, base[c] + fades[c] * spread(carry[:, lanes(c)]))

    def own_tile(g, u):
        c = g * UNITS + u
        lane = lanes(c)
        rates = rates_ref[:, lane]
        before, _ = scanned(states_of(1, c), rates)
        into = carry[:, lane]
        into = jnp.where(chip == 1, jnp.exp(-rates * float(half)) * into + first[:, lane], into)
        state = spread(weights(lane, rates)) * (before + jnp.exp(-spread(rates) * spots) * spread(into))
        gates(1, g, u)
        near(1, c)
        emit(c, state)

    def restore(into, g):
        cols = group(g)
        into[:, cols] = jnp.dot(back[...], gp[:, cols], preferred_element_type=F32).astype(BF16)

    halo_copy = pltpu.make_async_remote_copy(
        src_ref=halo_out, dst_ref=halo_in, send_sem=halo_sem.at[0], recv_sem=halo_sem.at[1],
        device_id=(lax.rem(me + 1, n_ctx), tp), device_id_type=MESH,
    )

    def twin_copy(g):
        return pltpu.make_async_remote_copy(
            src_ref=st_out.at[:, group(g)], dst_ref=twin_in.at[:, group(g)],
            send_sem=twin_send.at[g], recv_sem=twin_recv.at[g],
            device_id=(twin, tp), device_id_type=MESH,
        )

    def state_copy(g, src, dst):
        return pltpu.make_async_remote_copy(
            src_ref=both_out.at[:, group(g)], dst_ref=st_in.at[src, :, group(g)],
            send_sem=st_send.at[dst, g], recv_sem=st_recv.at[src, g],
            device_id=(dst * 2 + odd, tp), device_id_type=MESH,
        )

    def send_both(g):
        cols = group(g)
        twin_copy(g).wait_recv()
        other = twin_in[:, cols].astype(F32)
        own = own_end[:, cols]
        fade = decay_all[:, cols]
        total = jnp.where(odd == 1, fade * other + own, fade * own + other)
        both_out[:, cols] = total.astype(BF16)

        @pl.loop(pair + 1, n_ctx // 2)
        def _(dst):
            state_copy(g, pair, dst).start()

    rates_copy.wait()
    res_copy.wait()

    @pl.loop(0, tiles // 2)
    def _(k):
        responses(2 * k)
        responses(2 * k + 1)

    first_sent = jnp.where(odd == 1, FIRST[1], FIRST[0])
    second = jnp.where(odd == 1, SECOND[1], SECOND[0])
    tail_copy.wait()
    for j in range(3):
        halo_out[2 * j : 2 * j + 2, :] = tails[j].astype(F32)[TAIL - 2 :]
    halo_out[6:8, :] = jnp.zeros((2, channels), F32)
    taps_copy.wait()
    x_copy(0).wait()
    reorder(0, 0)

    pl.semaphore_wait(barrier, n_ctx + 1)

    @pl.when(me < n_ctx - 1)
    def _():
        halo_copy.start()

    @pl.loop(0, groups)
    def _(g):
        @pl.when(g < groups - 1)
        def _():
            x_copy(g + 1).wait()

        reorder(g, 1)
        last = ends(g, 1, ends(g, 0))
        reorder((g + 1) % groups, 0)
        ends(g, 3, ends(g, 2, last))

        @pl.when(g == HALO_GROUP)
        def _():
            @pl.when(me == 0)
            def _():
                halo_in[...] = jnp.zeros_like(halo_in)

            @pl.when(me > 0)
            def _():
                halo_copy.wait_recv()

        low = jnp.where(g == HALO_GROUP, 0, g)
        high = jnp.where(g < HALO_GROUP, low, g + 1)

        @pl.loop(low, high)
        def _(k):
            for u in range(UNITS):
                finish(k, u)
            twin_copy(k).start()

    @pl.loop(0, groups)
    def _(g):
        for u in range(UNITS):
            ahead(g, u)

        low = jnp.where(g == second, groups - 1, 0)
        high = jnp.where(g == second, groups, jnp.where(g == first_sent, groups - 1, 0))

        @pl.loop(low, high)
        def _(k):
            send_both(k)


    @pl.loop(0, groups)
    def _(g):
        cols = group(g)
        carry[:, cols] = jnp.zeros((modes, gwidth), F32)

        @pl.loop(0, pair)
        def _(src):
            fade = decay_all[:, cols] * decay_all[:, cols]
            state_copy(g, src, pair).wait_recv()
            carry[:, cols] = fade * carry[:, cols] + st_in[src, :, cols].astype(F32)

        @pl.when(odd == 1)
        def _():
            carry[:, cols] = decay_all[:, cols] * carry[:, cols] + twin_in[:, cols].astype(F32)

        for u in range(UNITS):
            carried_tile(g * UNITS + u)
        restore(ga, g)

    w_copy.wait()

    def to_sibling(n, out, into, send, recv):
        return pltpu.make_async_remote_copy(
            src_ref=out.at[n], dst_ref=into.at[n], send_sem=send.at[n], recv_sem=recv.at[n],
            device_id=(me, sibling), device_id_type=MESH,
        )

    def pair_copy(n):
        return to_sibling(n, pair_out, pair_in, pair_send, pair_recv)

    def own_copy(n):
        return to_sibling(n, own_out, own_in, own_send, own_recv)

    def far_copy(n):
        return pltpu.make_async_remote_copy(
            src_ref=far_out.at[n], dst_ref=far_in.at[n],
            send_sem=far_send.at[n], recv_sem=far_recv.at[n],
            device_id=(me, opposite), device_id_type=MESH,
        )

    mine = pl.ds(pl.multiple_of(core * share, share), share)
    theirs = pl.ds(pl.multiple_of((1 - core) * share, share), share)

    def forward(n):
        pair_copy(n).wait_recv()
        far_out[n] = (keep[n] + pair_in[n].astype(F32)).astype(BF16)
        far_copy(n).start()

    def columns(n):
        return pl.ds(pl.multiple_of(n * WIDTH, WIDTH), WIDTH)

    @pl.loop(0, n_out)
    def _(n):
        pt[...] = jnp.dot(ga[...], wv[:, columns(n)], preferred_element_type=F32)
        pair_out[n] = pt[theirs, :].astype(BF16)
        pair_copy(n).start()
        keep[n] = pt[mine, :]

        @pl.when(n >= LAG)
        def _():
            forward(n - LAG)

    @pl.loop(n_out - LAG, n_out)
    def _(n):
        forward(n)

    @pl.loop(0, groups)
    def _(g):
        for u in range(UNITS):
            own_tile(g, u)
        restore(gb, g)

    @pl.loop(0, n_out)
    def _(n):
        pt[...] = jnp.dot(gb[...], wv[:, columns(n)], preferred_element_type=F32)
        own_out[n] = pt[theirs, :].astype(BF16)
        own_copy(n).start()
        kept[n] = pt[mine, :]

    @pl.loop(0, n_out)
    def _(n):
        own_copy(n).wait_recv()
        far_copy(n).wait_recv()
        total = kept[n] + own_in[n].astype(F32) + far_in[n].astype(F32)
        out_ref[:, columns(n)] = total.astype(BF16)

    @pl.loop(0, n_out)
    def _(n):
        pair_copy(n).wait_send()
        own_copy(n).wait_send()
        far_copy(n).wait_send()

    @pl.loop(0, groups)
    def _(g):
        twin_copy(g).wait_send()

        @pl.loop(pair + 1, n_ctx // 2)
        def _(dst):
            state_copy(g, pair, dst).wait_send()

    @pl.when(me < n_ctx - 1)
    def _():
        halo_copy.wait_send()


def per_device(n_ctx, projections, short_filter, decay_rates, residues, out_weight):
    x = jnp.transpose(projections, (1, 0, 2))
    _, toks, channels = x.shape
    modes = decay_rates.shape[0]
    dout = out_weight.shape[1]
    tiles = channels // LANES
    groups = tiles // UNITS
    n_out = dout // WIDTH
    share = toks // 4
    half = toks // 2
    step = half // CHUNKS
    rows = half + 2 * CHUNKS
    dma = pltpu.SemaphoreType.DMA
    hbm = pl.BlockSpec(memory_space=pltpu.HBM)
    operands = [
        pltpu.with_memory_space_constraint(a, pltpu.HBM)
        for a in (x, short_filter, decay_rates, residues, out_weight)
    ]
    return pl.pallas_call(
        functools.partial(kernel, n_ctx),
        out_shape=jax.ShapeDtypeStruct((share, dout), BF16),
        in_specs=[hbm] * 5,
        out_specs=pl.BlockSpec(memory_space=pltpu.VMEM),
        scratch_shapes=[
            pltpu.VMEM((3, toks, channels), BF16),
            pltpu.VMEM((3, TAIL, channels), BF16),
            pltpu.VMEM(short_filter.shape, F32),
            pltpu.VMEM((modes, channels), F32),
            pltpu.VMEM((modes, channels), F32),
            pltpu.VMEM((2 * rows, toks), BF16),
            pltpu.VMEM((half, half), BF16),
            pltpu.VMEM((3, 2, tiles // 2, rows, LANES), F32),
            pltpu.VMEM((3, 2, tiles // 2, rows, LANES), F32),
            pltpu.VMEM((2, tiles, half, LANES), F32),
            pltpu.VMEM((tiles, half, LANES), F32),
            pltpu.VMEM((tiles, half, LANES), F32),
            pltpu.VMEM((half, channels), BF16),
            pltpu.VMEM((half, channels), BF16),
            pltpu.VMEM((half, channels), BF16),
            pltpu.VMEM((channels, dout), BF16),
            pltpu.VMEM((half, WIDTH), F32),
            pltpu.VMEM((2, tiles, modes * CHUNKS, LANES), F32),
            pltpu.VMEM((tiles, modes, CHUNKS, LANES), F32),
            pltpu.VMEM((tiles, modes, CHUNKS, LANES), F32),
            pltpu.VMEM((tiles, step, LANES), F32),
            pltpu.VMEM((8, channels), F32),
            pltpu.VMEM((8, channels), F32),
            pltpu.VMEM((modes, channels), BF16),
            pltpu.VMEM((modes, channels), BF16),
            pltpu.VMEM((modes, channels), BF16),
            pltpu.VMEM((n_ctx // 2, modes, channels), BF16),
            pltpu.VMEM((modes, channels), F32),
            pltpu.VMEM((modes, channels), F32),
            pltpu.VMEM((modes, channels), F32),
            pltpu.VMEM((modes, channels), F32),
            pltpu.VMEM((n_out, share, WIDTH), F32),
            pltpu.VMEM((n_out, share, WIDTH), F32),
            pltpu.VMEM((n_out, share, WIDTH), BF16),
            pltpu.VMEM((n_out, share, WIDTH), BF16),
            pltpu.VMEM((n_out, share, WIDTH), BF16),
            pltpu.VMEM((n_out, share, WIDTH), BF16),
            pltpu.VMEM((n_out, share, WIDTH), BF16),
            pltpu.VMEM((n_out, share, WIDTH), BF16),
            dma((groups,)), dma((4,)), dma, dma((2,)),
            dma((groups,)), dma((groups,)),
            dma((n_ctx // 2, groups)), dma((n_ctx // 2, groups)),
            dma((n_out,)), dma((n_out,)), dma((n_out,)), dma((n_out,)),
            dma((n_out,)), dma((n_out,)),
        ],
        compiler_params=pltpu.CompilerParams(
            collective_id=0, has_side_effects=True, vmem_limit_bytes=48 * 2**20
        ),
    )(*operands)


def solution(mesh):
    placed = (
        P("ctx", None, "tp"),
        P(None, None, "tp"),
        P(None, "tp"),
        P(None, "tp"),
        P("tp", None),
    )
    return jax.shard_map(
        functools.partial(per_device, mesh.shape["ctx"]),
        mesh=mesh, in_specs=placed, out_specs=P(("ctx", "tp"), None), check_vma=False,
    )
```

```python
import functools

import jax
import jax.numpy as jnp
from jax import lax
from jax.experimental import pallas as pl
from jax.experimental.pallas import tpu as pltpu
from jax.sharding import PartitionSpec as P

LANES = 128
CHUNKS = 8
UNITS = 4
HALO_GROUP = 2
MXU = 256
WIDTH = 512
FIRST = (1, 0)
SECOND = (2, 1)
LAG = 2
TAIL = 16
MESH = pl.DeviceIdType.MESH
F32 = jnp.float32
BF16 = jnp.bfloat16


def summed(terms):
    while terms.shape[0] % 2 == 0:
        middle = terms.shape[0] // 2
        terms = terms[:middle] + terms[middle:]
    return jnp.sum(terms, axis=0)


def kernel(
    n_ctx, x_hbm, taps_hbm, rates_hbm, res_hbm, w_hbm, out_ref,
    xb, tails, taps_ref, rates_ref, res_ref, order, back, xs_even, xs_odd, pf, qf, yl, gp, ga, gb, wv, pt, raw, base, fades, entry, hb,
    halo_out, halo_in, st_out, twin_in, both_out, st_in,
    own_end, decay_all, carry, first, keep, kept, pair_out, pair_in, own_out, own_in, far_out, far_in,
    x_sem, in_sem, w_sem, halo_sem, twin_send, twin_recv, st_send, st_recv,
    pair_send, pair_recv, own_send, own_recv, far_send, far_recv,
):
    me = lax.axis_index("ctx")
    tp = lax.axis_index("tp")
    pair, odd = me // 2, me % 2
    twin = pair * 2 + (1 - odd)
    chip, core = tp // 2, tp % 2
    sibling = chip * 2 + (1 - core)
    opposite = (1 - chip) * 2 + core
    toks, channels = xb.shape[1], xb.shape[2]
    modes = rates_ref.shape[0]
    half = toks // 2
    step = half // CHUNKS
    rows = half + 2 * CHUNKS
    gwidth = UNITS * LANES
    tiles = channels // LANES
    groups = channels // gwidth
    per_block = MXU // LANES
    n_out = w_hbm.shape[1] // WIDTH
    share = toks // 4
    early = 1 - chip

    def group(g):
        return pl.ds(pl.multiple_of(g * gwidth, gwidth), gwidth)

    def x_copy(g):
        return pltpu.make_async_copy(x_hbm.at[:, :, group(g)], xb.at[:, :, group(g)], x_sem.at[g])

    tail_copy = pltpu.make_async_copy(x_hbm.at[:, toks - TAIL :, :], tails, in_sem.at[0])
    rates_copy = pltpu.make_async_copy(rates_hbm, rates_ref, in_sem.at[1])
    taps_copy = pltpu.make_async_copy(taps_hbm, taps_ref, in_sem.at[2])
    res_copy = pltpu.make_async_copy(res_hbm, res_ref, in_sem.at[3])
    w_copy = pltpu.make_async_copy(w_hbm, wv, w_sem)

    rates_copy.start()
    res_copy.start()
    x_copy(0).start()
    taps_copy.start()
    tail_copy.start()

    @pl.loop(1, groups)
    def _(g):
        x_copy(g).start()

    w_copy.start()

    barrier = pltpu.get_barrier_semaphore()

    @pl.loop(1, n_ctx)
    def _(k):
        pl.semaphore_signal(
            barrier, inc=1, device_id=(lax.rem(me + k, n_ctx), tp), device_id_type=MESH
        )

    for other in (sibling, opposite):
        pl.semaphore_signal(barrier, inc=1, device_id=(me, other), device_id_type=MESH)

    for b in range(2):
        row = lax.broadcasted_iota(jnp.int32, (rows, toks), 0)
        token = lax.broadcasted_iota(jnp.int32, (rows, toks), 1)
        start = early * half if b == 0 else chip * half
        wanted = start + (row % CHUNKS) * step + row // CHUNKS - 2
        order[b * rows : (b + 1) * rows, :] = jnp.where(token == wanted, 1.0, 0.0).astype(BF16)
    token = lax.broadcasted_iota(jnp.int32, (half, half), 0)
    row = lax.broadcasted_iota(jnp.int32, (half, half), 1)
    back[...] = jnp.where(token == (row % CHUNKS) * step + row // CHUNKS, 1.0, 0.0).astype(BF16)

    place = lax.broadcasted_iota(jnp.int32, (1, CHUNKS, LANES), 1)
    late_block = jnp.where(chip == 0, 1.0, 0.0).astype(F32)

    def spread(values):
        return jnp.broadcast_to(values[:, None, :], (values.shape[0], CHUNKS, LANES))

    def lanes(c):
        return pl.ds(pl.multiple_of(c * LANES, LANES), LANES)

    def collapse(terms):
        spot = place[0]
        out = []
        for f in range(0, len(terms), CHUNKS):
            v = terms[f : f + CHUNKS]
            low = spot < 4
            y = [
                jnp.where(low, v[n], v[n + 4]) + pltpu.roll(jnp.where(low, v[n + 4], v[n]), 4, 0)
                for n in range(4)
            ]
            low = spot % 4 < 2
            z = [
                jnp.where(low, y[n] + pltpu.roll(y[n], 6, 0), y[n + 2] + pltpu.roll(y[n + 2], 2, 0))
                for n in range(2)
            ]
            low = spot % 2 == 0
            out.append(jnp.where(low, z[0] + pltpu.roll(z[0], 7, 0), z[1] + pltpu.roll(z[1], 1, 0)))
        return jnp.concatenate(out, axis=0)

    def ordered(g, u):
        return (xs_even, xs_odd)[u // per_block], g * per_block + u % per_block

    def reorder(g, which):
        cols = pl.ds(pl.multiple_of(g * gwidth + which * MXU, MXU), MXU)
        for j in range(3):
            moved = jnp.dot(order[...], xb[j, :, cols], preferred_element_type=F32)
            for b in range(2):
                for u in range(which * per_block, (which + 1) * per_block):
                    xs, at = ordered(g, u)
                    left = u % per_block * LANES
                    xs[j, b, at] = moved[b * rows : (b + 1) * rows, left : left + LANES]

    def feature(j, b, g, u, low, high):
        lane = lanes(g * UNITS + u)
        xs, where = ordered(g, u)
        total = None
        for i in range(3):
            at = (2 - i) * CHUNKS
            term = taps_ref[i, j : j + 1, lane] * xs[j, b, where, at + low : at + high, :]
            total = term if total is None else total + term
        return total

    def add_halo(j, g, u):
        lane = lanes(g * UNITS + u)
        xs, where = ordered(g, u)
        xs[j, early, where, 0:1, :] = halo_in[2 * j : 2 * j + 1, lane]
        xs[j, early, where, CHUNKS : CHUNKS + 1, :] = halo_in[2 * j + 1 : 2 * j + 2, lane]

    def chunk(b, c, s):
        return raw[b, c, s * (modes + 1) : s * (modes + 1) + modes, :]

    def ends(g, u, last=None):
        c = g * UNITS + u
        decay = jnp.exp(-spread(rates_ref[:, lanes(c)]))
        for b in range(2):
            product = feature(1, b, g, u, 0, half) * feature(2, b, g, u, 0, half)
            pf[b, c] = product
            opening = product[:CHUNKS]
            if last is not None:
                opening = opening + 0.0 * last
            state = jnp.broadcast_to(opening[None], (modes, CHUNKS, LANES))
            for i in range(1, step):
                state = decay * state + product[None, i * CHUNKS : (i + 1) * CHUNKS]
            for n in range(modes):
                raw[b, c, pl.ds(n, CHUNKS, stride=modes + 1), :] = state[n]
            last = state[modes - 1]
        return last

    def finish(g, u):
        c = g * UNITS + u
        lane = lanes(c)
        rates = rates_ref[:, lane]
        two = 2 * CHUNKS
        for j in (1, 2):
            add_halo(j, g, u)
        product = feature(1, early, g, u, 0, two) * feature(2, early, g, u, 0, two)
        change = product - pf[early, c, :two, :]
        pf[early, c, :two, :] = product
        grown = jnp.exp(-rates) * change[:1] + change[CHUNKS : CHUNKS + 1]
        end = chunk(early, c, 0) + jnp.exp(-rates * float(step - 2)) * grown
        raw[early, c, 0:modes, :] = end
        fade = jnp.exp(-rates * float(step))
        for s in range(1, CHUNKS):
            end = fade * end + chunk(early, c, s)
        first[:, lane] = end
        for s in range(CHUNKS):
            end = fade * end + chunk(chip, c, s)
        own_end[:, lane] = end
        st_out[:, lane] = end.astype(BF16)

    def near(b, c):
        for i in range(step):
            total = None
            for k in range(i + 1):
                at = (i - k) * CHUNKS
                term = hb[c, k : k + 1, :] * pf[b, c, at : at + CHUNKS, :]
                total = term if total is None else total + term
            yl[c, i * CHUNKS : (i + 1) * CHUNKS, :] = total

    def responses(c):
        lane = lanes(c)
        rates = rates_ref[:, lane]
        decay = jnp.exp(-rates)
        now = res_ref[:, lane] * jnp.sqrt(2.0 * rates)
        terms = []
        for i in range(step):
            terms.append(summed(now.reshape(modes // CHUNKS, CHUNKS, LANES)))
            now = now * decay
        hb[c] = collapse(terms)
        decay_all[:, lane] = jnp.exp(-rates * float(toks))

    def gates(b, g, u):
        if b == 0:
            add_halo(0, g, u)
        qf[g * UNITS + u] = feature(0, b, g, u, 0, half)

    def weights(lane, rates):
        return res_ref[:, lane] * jnp.sqrt(2.0 * rates) * jnp.exp(-rates)

    def ahead(g, u):
        c = g * UNITS + u
        lane = lanes(c)
        rates = rates_ref[:, lane]
        weight = weights(lane, rates)
        fade = jnp.exp(-rates * float(step))
        state = first[:, lane] * late_block
        reach = weight * jnp.exp(-rates * (float(half) * late_block))
        for s in range(CHUNKS):
            base[c, s] = weight * state
            fades[c, s] = reach
            if s < CHUNKS - 1:
                state = fade * state + chunk(0, c, s)
                reach = fade * reach
        gates(0, g, u)
        near(0, c)

    def enter(u, s, state):
        entry[u, pl.ds(s, modes, stride=CHUNKS + 1), :] = state

    def emit(c, u):
        lane = lanes(c)
        decay = spread(jnp.exp(-rates_ref[:, lane]))
        state = [entry[u, n * (CHUNKS + 1) : n * (CHUNKS + 1) + CHUNKS, :] for n in range(modes)]
        for i in range(0, step, 2):
            parts = []
            for k in (i, i + 1):
                at = slice(k * CHUNKS, (k + 1) * CHUNKS)
                terms = state
                while len(terms) > 1:
                    middle = len(terms) // 2
                    terms = [terms[n] + terms[n + middle] for n in range(middle)]
                parts.append(qf[c, at, :] * (yl[c, at, :] + terms[0]))
                state = [decay[n] * state[n] for n in range(modes)]
            gp[i * CHUNKS : (i + 2) * CHUNKS, lane] = jnp.concatenate(parts, axis=0).astype(BF16)

    def carried_tile(g, u):
        c = g * UNITS + u
        into = carry[:, lanes(c)]
        for s in range(CHUNKS):
            enter(u, s, base[c, s] + fades[c, s] * into)
        emit(c, u)

    def own_tile(g, u):
        c = g * UNITS + u
        lane = lanes(c)
        rates = rates_ref[:, lane]
        weight = weights(lane, rates)
        fade = jnp.exp(-rates * float(step))
        state = carry[:, lane]
        state = jnp.where(chip == 1, jnp.exp(-rates * float(half)) * state + first[:, lane], state)
        for s in range(CHUNKS):
            enter(u, s, weight * state)
            if s < CHUNKS - 1:
                state = fade * state + chunk(1, c, s)
        gates(1, g, u)
        near(1, c)
        emit(c, u)

    def restore(into, g):
        cols = group(g)
        into[:, cols] = jnp.dot(back[...], gp[:, cols], preferred_element_type=F32).astype(BF16)

    halo_copy = pltpu.make_async_remote_copy(
        src_ref=halo_out, dst_ref=halo_in, send_sem=halo_sem.at[0], recv_sem=halo_sem.at[1],
        device_id=(lax.rem(me + 1, n_ctx), tp), device_id_type=MESH,
    )

    def twin_copy(g):
        return pltpu.make_async_remote_copy(
            src_ref=st_out.at[:, group(g)], dst_ref=twin_in.at[:, group(g)],
            send_sem=twin_send.at[g], recv_sem=twin_recv.at[g],
            device_id=(twin, tp), device_id_type=MESH,
        )

    def state_copy(g, src, dst):
        return pltpu.make_async_remote_copy(
            src_ref=both_out.at[:, group(g)], dst_ref=st_in.at[src, :, group(g)],
            send_sem=st_send.at[dst, g], recv_sem=st_recv.at[src, g],
            device_id=(dst * 2 + odd, tp), device_id_type=MESH,
        )

    def send_both(g):
        cols = group(g)
        twin_copy(g).wait_recv()
        other = twin_in[:, cols].astype(F32)
        own = own_end[:, cols]
        fade = decay_all[:, cols]
        total = jnp.where(odd == 1, fade * other + own, fade * own + other)
        both_out[:, cols] = total.astype(BF16)

        @pl.loop(pair + 1, n_ctx // 2)
        def _(dst):
            state_copy(g, pair, dst).start()

    rates_copy.wait()
    res_copy.wait()

    @pl.loop(0, tiles // 2)
    def _(k):
        responses(2 * k)
        responses(2 * k + 1)

    first_sent = jnp.where(odd == 1, FIRST[1], FIRST[0])
    second = jnp.where(odd == 1, SECOND[1], SECOND[0])
    tail_copy.wait()
    for j in range(3):
        halo_out[2 * j : 2 * j + 2, :] = tails[j].astype(F32)[TAIL - 2 :]
    halo_out[6:8, :] = jnp.zeros((2, channels), F32)
    taps_copy.wait()
    x_copy(0).wait()
    reorder(0, 0)

    pl.semaphore_wait(barrier, n_ctx + 1)

    @pl.when(me < n_ctx - 1)
    def _():
        halo_copy.start()

    @pl.loop(0, groups)
    def _(g):
        @pl.when(g < groups - 1)
        def _():
            x_copy(g + 1).wait()

        reorder(g, 1)
        last = ends(g, 1, ends(g, 0))
        reorder((g + 1) % groups, 0)
        ends(g, 3, ends(g, 2, last))

        @pl.when(g == HALO_GROUP)
        def _():
            @pl.when(me == 0)
            def _():
                halo_in[...] = jnp.zeros_like(halo_in)

            @pl.when(me > 0)
            def _():
                halo_copy.wait_recv()

        low = jnp.where(g == HALO_GROUP, 0, g)
        high = jnp.where(g < HALO_GROUP, low, g + 1)

        @pl.loop(low, high)
        def _(k):
            for u in range(UNITS):
                finish(k, u)
            twin_copy(k).start()

    @pl.loop(0, groups)
    def _(g):
        for u in range(UNITS):
            ahead(g, u)

        low = jnp.where(g == second, groups - 1, 0)
        high = jnp.where(g == second, groups, jnp.where(g == first_sent, groups - 1, 0))

        @pl.loop(low, high)
        def _(k):
            send_both(k)


    @pl.loop(0, groups)
    def _(g):
        cols = group(g)
        carry[:, cols] = jnp.zeros((modes, gwidth), F32)

        @pl.loop(0, pair)
        def _(src):
            fade = decay_all[:, cols] * decay_all[:, cols]
            state_copy(g, src, pair).wait_recv()
            carry[:, cols] = fade * carry[:, cols] + st_in[src, :, cols].astype(F32)

        @pl.when(odd == 1)
        def _():
            carry[:, cols] = decay_all[:, cols] * carry[:, cols] + twin_in[:, cols].astype(F32)

        for u in range(UNITS):
            carried_tile(g, u)
        restore(ga, g)

    w_copy.wait()

    def to_sibling(n, out, into, send, recv):
        return pltpu.make_async_remote_copy(
            src_ref=out.at[n], dst_ref=into.at[n], send_sem=send.at[n], recv_sem=recv.at[n],
            device_id=(me, sibling), device_id_type=MESH,
        )

    def pair_copy(n):
        return to_sibling(n, pair_out, pair_in, pair_send, pair_recv)

    def own_copy(n):
        return to_sibling(n, own_out, own_in, own_send, own_recv)

    def far_copy(n):
        return pltpu.make_async_remote_copy(
            src_ref=far_out.at[n], dst_ref=far_in.at[n],
            send_sem=far_send.at[n], recv_sem=far_recv.at[n],
            device_id=(me, opposite), device_id_type=MESH,
        )

    mine = pl.ds(pl.multiple_of(core * share, share), share)
    theirs = pl.ds(pl.multiple_of((1 - core) * share, share), share)

    def forward(n):
        pair_copy(n).wait_recv()
        far_out[n] = (keep[n] + pair_in[n].astype(F32)).astype(BF16)
        far_copy(n).start()

    def columns(n):
        return pl.ds(pl.multiple_of(n * WIDTH, WIDTH), WIDTH)

    @pl.loop(0, n_out)
    def _(n):
        pt[...] = jnp.dot(ga[...], wv[:, columns(n)], preferred_element_type=F32)
        pair_out[n] = pt[theirs, :].astype(BF16)
        pair_copy(n).start()
        keep[n] = pt[mine, :]

        @pl.when(n >= LAG)
        def _():
            forward(n - LAG)

    @pl.loop(n_out - LAG, n_out)
    def _(n):
        forward(n)

    @pl.loop(0, groups)
    def _(g):
        for u in range(UNITS):
            own_tile(g, u)
        restore(gb, g)

    @pl.loop(0, n_out)
    def _(n):
        pt[...] = jnp.dot(gb[...], wv[:, columns(n)], preferred_element_type=F32)
        own_out[n] = pt[theirs, :].astype(BF16)
        own_copy(n).start()
        kept[n] = pt[mine, :]

    @pl.loop(0, n_out)
    def _(n):
        own_copy(n).wait_recv()
        far_copy(n).wait_recv()
        total = kept[n] + own_in[n].astype(F32) + far_in[n].astype(F32)
        out_ref[:, columns(n)] = total.astype(BF16)

    @pl.loop(0, n_out)
    def _(n):
        pair_copy(n).wait_send()
        own_copy(n).wait_send()
        far_copy(n).wait_send()

    @pl.loop(0, groups)
    def _(g):
        twin_copy(g).wait_send()

        @pl.loop(pair + 1, n_ctx // 2)
        def _(dst):
            state_copy(g, pair, dst).wait_send()

    @pl.when(me < n_ctx - 1)
    def _():
        halo_copy.wait_send()


def per_device(n_ctx, projections, short_filter, decay_rates, residues, out_weight):
    x = jnp.transpose(projections, (1, 0, 2))
    _, toks, channels = x.shape
    modes = decay_rates.shape[0]
    dout = out_weight.shape[1]
    tiles = channels // LANES
    groups = tiles // UNITS
    n_out = dout // WIDTH
    share = toks // 4
    half = toks // 2
    step = half // CHUNKS
    rows = half + 2 * CHUNKS
    dma = pltpu.SemaphoreType.DMA
    hbm = pl.BlockSpec(memory_space=pltpu.HBM)
    operands = [
        pltpu.with_memory_space_constraint(a, pltpu.HBM)
        for a in (x, short_filter, decay_rates, residues, out_weight)
    ]
    return pl.pallas_call(
        functools.partial(kernel, n_ctx),
        out_shape=jax.ShapeDtypeStruct((share, dout), BF16),
        in_specs=[hbm] * 5,
        out_specs=pl.BlockSpec(memory_space=pltpu.VMEM),
        scratch_shapes=[
            pltpu.VMEM((3, toks, channels), BF16),
            pltpu.VMEM((3, TAIL, channels), BF16),
            pltpu.VMEM(short_filter.shape, F32),
            pltpu.VMEM((modes, channels), F32),
            pltpu.VMEM((modes, channels), F32),
            pltpu.VMEM((2 * rows, toks), BF16),
            pltpu.VMEM((half, half), BF16),
            pltpu.VMEM((3, 2, tiles // 2, rows, LANES), F32),
            pltpu.VMEM((3, 2, tiles // 2, rows, LANES), F32),
            pltpu.VMEM((2, tiles, half, LANES), F32),
            pltpu.VMEM((tiles, half, LANES), F32),
            pltpu.VMEM((tiles, half, LANES), F32),
            pltpu.VMEM((half, channels), BF16),
            pltpu.VMEM((half, channels), BF16),
            pltpu.VMEM((half, channels), BF16),
            pltpu.VMEM((channels, dout), BF16),
            pltpu.VMEM((half, WIDTH), F32),
            pltpu.VMEM((2, tiles, CHUNKS * (modes + 1), LANES), F32),
            pltpu.VMEM((tiles, CHUNKS, modes, LANES), F32),
            pltpu.VMEM((tiles, CHUNKS, modes, LANES), F32),
            pltpu.VMEM((UNITS, modes * (CHUNKS + 1), LANES), F32),
            pltpu.VMEM((tiles, step, LANES), F32),
            pltpu.VMEM((8, channels), F32),
            pltpu.VMEM((8, channels), F32),
            pltpu.VMEM((modes, channels), BF16),
            pltpu.VMEM((modes, channels), BF16),
            pltpu.VMEM((modes, channels), BF16),
            pltpu.VMEM((n_ctx // 2, modes, channels), BF16),
            pltpu.VMEM((modes, channels), F32),
            pltpu.VMEM((modes, channels), F32),
            pltpu.VMEM((modes, channels), F32),
            pltpu.VMEM((modes, channels), F32),
            pltpu.VMEM((n_out, share, WIDTH), F32),
            pltpu.VMEM((n_out, share, WIDTH), F32),
            pltpu.VMEM((n_out, share, WIDTH), BF16),
            pltpu.VMEM((n_out, share, WIDTH), BF16),
            pltpu.VMEM((n_out, share, WIDTH), BF16),
            pltpu.VMEM((n_out, share, WIDTH), BF16),
            pltpu.VMEM((n_out, share, WIDTH), BF16),
            pltpu.VMEM((n_out, share, WIDTH), BF16),
            dma((groups,)), dma((4,)), dma, dma((2,)),
            dma((groups,)), dma((groups,)),
            dma((n_ctx // 2, groups)), dma((n_ctx // 2, groups)),
            dma((n_out,)), dma((n_out,)), dma((n_out,)), dma((n_out,)),
            dma((n_out,)), dma((n_out,)),
        ],
        compiler_params=pltpu.CompilerParams(
            collective_id=0, has_side_effects=True, vmem_limit_bytes=48 * 2**20
        ),
    )(*operands)


def solution(mesh):
    placed = (
        P("ctx", None, "tp"),
        P(None, None, "tp"),
        P(None, "tp"),
        P(None, "tp"),
        P("tp", None),
    )
    return jax.shard_map(
        functools.partial(per_device, mesh.shape["ctx"]),
        mesh=mesh, in_specs=placed, out_specs=P(("ctx", "tp"), None), check_vma=False,
    )
```

```python
import functools

import jax
import jax.numpy as jnp
from jax import lax
from jax.experimental import pallas as pl
from jax.experimental.pallas import tpu as pltpu
from jax.sharding import PartitionSpec as P

LANES = 128
CHUNKS = 8
UNITS = 4
HALO_GROUP = 3
MXU = 256
WIDTH = 512
FIRST = (2, 2)
SECOND = (3, 3)
LAG = 2
TAIL = 16
MESH = pl.DeviceIdType.MESH
F32 = jnp.float32
BF16 = jnp.bfloat16


def summed(terms):
    while terms.shape[0] % 2 == 0:
        middle = terms.shape[0] // 2
        terms = terms[:middle] + terms[middle:]
    return jnp.sum(terms, axis=0)


def kernel(
    n_ctx, x_hbm, taps_hbm, rates_hbm, res_hbm, w_hbm, out_ref,
    xb, tails, taps_ref, rates_ref, res_ref, order, back, xs_even, xs_odd, pf, qf, yl, gp, ga, gb, wv, pt, raw, base, fades, entry, hb,
    halo_out, halo_in, st_out, twin_in, both_out, st_in,
    own_end, decay_all, carry, first, keep, kept, pair_out, pair_in, own_out, own_in, far_out, far_in,
    x_sem, in_sem, w_sem, halo_sem, twin_send, twin_recv, st_send, st_recv,
    pair_send, pair_recv, own_send, own_recv, far_send, far_recv,
):
    me = lax.axis_index("ctx")
    tp = lax.axis_index("tp")
    pair, odd = me // 2, me % 2
    twin = pair * 2 + (1 - odd)
    chip, core = tp // 2, tp % 2
    sibling = chip * 2 + (1 - core)
    opposite = (1 - chip) * 2 + core
    toks, channels = xb.shape[1], xb.shape[2]
    modes = rates_ref.shape[0]
    half = toks // 2
    step = half // CHUNKS
    rows = half + 2 * CHUNKS
    gwidth = UNITS * LANES
    tiles = channels // LANES
    groups = channels // gwidth
    per_block = MXU // LANES
    n_out = w_hbm.shape[1] // WIDTH
    share = toks // 4
    early = 1 - chip

    def group(g):
        return pl.ds(pl.multiple_of(g * gwidth, gwidth), gwidth)

    def x_copy(g):
        return pltpu.make_async_copy(x_hbm.at[:, :, group(g)], xb.at[:, :, group(g)], x_sem.at[g])

    tail_copy = pltpu.make_async_copy(x_hbm.at[:, toks - TAIL :, :], tails, in_sem.at[0])
    rates_copy = pltpu.make_async_copy(rates_hbm, rates_ref, in_sem.at[1])
    taps_copy = pltpu.make_async_copy(taps_hbm, taps_ref, in_sem.at[2])
    res_copy = pltpu.make_async_copy(res_hbm, res_ref, in_sem.at[3])
    w_copy = pltpu.make_async_copy(w_hbm, wv, w_sem)

    rates_copy.start()
    res_copy.start()
    x_copy(0).start()
    taps_copy.start()
    tail_copy.start()

    @pl.loop(1, groups)
    def _(g):
        x_copy(g).start()

    w_copy.start()

    barrier = pltpu.get_barrier_semaphore()

    @pl.loop(1, n_ctx)
    def _(k):
        pl.semaphore_signal(
            barrier, inc=1, device_id=(lax.rem(me + k, n_ctx), tp), device_id_type=MESH
        )

    for other in (sibling, opposite):
        pl.semaphore_signal(barrier, inc=1, device_id=(me, other), device_id_type=MESH)

    for b in range(2):
        row = lax.broadcasted_iota(jnp.int32, (rows, toks), 0)
        token = lax.broadcasted_iota(jnp.int32, (rows, toks), 1)
        start = early * half if b == 0 else chip * half
        wanted = start + (row % CHUNKS) * step + row // CHUNKS - 2
        order[b * rows : (b + 1) * rows, :] = jnp.where(token == wanted, 1.0, 0.0).astype(BF16)
    token = lax.broadcasted_iota(jnp.int32, (half, half), 0)
    row = lax.broadcasted_iota(jnp.int32, (half, half), 1)
    back[...] = jnp.where(token == (row % CHUNKS) * step + row // CHUNKS, 1.0, 0.0).astype(BF16)

    place = lax.broadcasted_iota(jnp.int32, (1, CHUNKS, LANES), 1)
    late_block = jnp.where(chip == 0, 1.0, 0.0).astype(F32)

    def spread(values):
        return jnp.broadcast_to(values[:, None, :], (values.shape[0], CHUNKS, LANES))

    def lanes(c):
        return pl.ds(pl.multiple_of(c * LANES, LANES), LANES)

    def collapse(terms):
        spot = place[0]
        out = []
        for f in range(0, len(terms), CHUNKS):
            v = terms[f : f + CHUNKS]
            low = spot < 4
            y = [
                jnp.where(low, v[n], v[n + 4]) + pltpu.roll(jnp.where(low, v[n + 4], v[n]), 4, 0)
                for n in range(4)
            ]
            low = spot % 4 < 2
            z = [
                jnp.where(low, y[n] + pltpu.roll(y[n], 6, 0), y[n + 2] + pltpu.roll(y[n + 2], 2, 0))
                for n in range(2)
            ]
            low = spot % 2 == 0
            out.append(jnp.where(low, z[0] + pltpu.roll(z[0], 7, 0), z[1] + pltpu.roll(z[1], 1, 0)))
        return jnp.concatenate(out, axis=0)

    def ordered(g, u):
        return (xs_even, xs_odd)[u // per_block], g * per_block + u % per_block

    def reorder(g, which):
        cols = pl.ds(pl.multiple_of(g * gwidth + which * MXU, MXU), MXU)
        for j in range(3):
            moved = jnp.dot(order[...], xb[j, :, cols], preferred_element_type=F32)
            for b in range(2):
                for u in range(which * per_block, (which + 1) * per_block):
                    xs, at = ordered(g, u)
                    left = u % per_block * LANES
                    xs[j, b, at] = moved[b * rows : (b + 1) * rows, left : left + LANES]

    def feature(j, b, g, u, low, high):
        lane = lanes(g * UNITS + u)
        xs, where = ordered(g, u)
        total = None
        for i in range(3):
            at = (2 - i) * CHUNKS
            term = taps_ref[i, j : j + 1, lane] * xs[j, b, where, at + low : at + high, :]
            total = term if total is None else total + term
        return total

    def add_halo(j, g, u):
        lane = lanes(g * UNITS + u)
        xs, where = ordered(g, u)
        xs[j, early, where, 0:1, :] = halo_in[2 * j : 2 * j + 1, lane]
        xs[j, early, where, CHUNKS : CHUNKS + 1, :] = halo_in[2 * j + 1 : 2 * j + 2, lane]

    def chunk(b, c, s):
        return raw[b, c, s * (modes + 1) : s * (modes + 1) + modes, :]

    def ends(g, u, last=None):
        c = g * UNITS + u
        decay = jnp.exp(-spread(rates_ref[:, lanes(c)]))
        for b in range(2):
            product = feature(1, b, g, u, 0, half) * feature(2, b, g, u, 0, half)
            pf[b, c] = product
            opening = product[:CHUNKS]
            if last is not None:
                opening = opening + 0.0 * last
            state = jnp.broadcast_to(opening[None], (modes, CHUNKS, LANES))
            for i in range(1, step):
                state = decay * state + product[None, i * CHUNKS : (i + 1) * CHUNKS]
            for n in range(modes):
                raw[b, c, pl.ds(n, CHUNKS, stride=modes + 1), :] = state[n]
            last = state[modes - 1]
        return last

    def finish(g, u):
        c = g * UNITS + u
        lane = lanes(c)
        rates = rates_ref[:, lane]
        two = 2 * CHUNKS
        for j in (1, 2):
            add_halo(j, g, u)
        product = feature(1, early, g, u, 0, two) * feature(2, early, g, u, 0, two)
        change = product - pf[early, c, :two, :]
        pf[early, c, :two, :] = product
        grown = jnp.exp(-rates) * change[:1] + change[CHUNKS : CHUNKS + 1]
        end = chunk(early, c, 0) + jnp.exp(-rates * float(step - 2)) * grown
        raw[early, c, 0:modes, :] = end
        fade = jnp.exp(-rates * float(step))
        for s in range(1, CHUNKS):
            end = fade * end + chunk(early, c, s)
        first[:, lane] = end
        for s in range(CHUNKS):
            end = fade * end + chunk(chip, c, s)
        own_end[:, lane] = end
        st_out[:, lane] = end.astype(BF16)

    def near(b, c):
        for i in range(step):
            total = None
            for k in range(i + 1):
                at = (i - k) * CHUNKS
                term = hb[c, k : k + 1, :] * pf[b, c, at : at + CHUNKS, :]
                total = term if total is None else total + term
            yl[c, i * CHUNKS : (i + 1) * CHUNKS, :] = total

    def responses(c):
        lane = lanes(c)
        rates = rates_ref[:, lane]
        decay = jnp.exp(-rates)
        now = res_ref[:, lane] * jnp.sqrt(2.0 * rates)
        terms = []
        for i in range(step):
            terms.append(summed(now.reshape(modes // CHUNKS, CHUNKS, LANES)))
            now = now * decay
        hb[c] = collapse(terms)
        decay_all[:, lane] = jnp.exp(-rates * float(toks))

    def gates(b, g, u):
        if b == 0:
            add_halo(0, g, u)
        qf[g * UNITS + u] = feature(0, b, g, u, 0, half)

    def weights(lane, rates):
        return res_ref[:, lane] * jnp.sqrt(2.0 * rates) * jnp.exp(-rates)

    def ahead(g, u):
        c = g * UNITS + u
        lane = lanes(c)
        rates = rates_ref[:, lane]
        weight = weights(lane, rates)
        fade = jnp.exp(-rates * float(step))
        state = first[:, lane] * late_block
        reach = weight * jnp.exp(-rates * (float(half) * late_block))
        for s in range(CHUNKS):
            base[c, s] = weight * state
            fades[c, s] = reach
            if s < CHUNKS - 1:
                state = fade * state + chunk(0, c, s)
                reach = fade * reach
        gates(0, g, u)
        near(0, c)

    def enter(u, s, state):
        entry[u, pl.ds(s, modes, stride=CHUNKS + 1), :] = state

    def emit(c, u):
        lane = lanes(c)
        decay = spread(jnp.exp(-rates_ref[:, lane]))
        state = [entry[u, n * (CHUNKS + 1) : n * (CHUNKS + 1) + CHUNKS, :] for n in range(modes)]
        for i in range(0, step, 2):
            parts = []
            for k in (i, i + 1):
                at = slice(k * CHUNKS, (k + 1) * CHUNKS)
                terms = state
                while len(terms) > 1:
                    middle = len(terms) // 2
                    terms = [terms[n] + terms[n + middle] for n in range(middle)]
                parts.append(qf[c, at, :] * (yl[c, at, :] + terms[0]))
                state = [decay[n] * state[n] for n in range(modes)]
            gp[i * CHUNKS : (i + 2) * CHUNKS, lane] = jnp.concatenate(parts, axis=0).astype(BF16)

    def carried_tile(g, u):
        c = g * UNITS + u
        into = carry[:, lanes(c)]
        for s in range(CHUNKS):
            enter(u, s, base[c, s] + fades[c, s] * into)
        emit(c, u)

    def own_tile(g, u):
        c = g * UNITS + u
        lane = lanes(c)
        rates = rates_ref[:, lane]
        weight = weights(lane, rates)
        fade = jnp.exp(-rates * float(step))
        state = carry[:, lane]
        state = jnp.where(chip == 1, jnp.exp(-rates * float(half)) * state + first[:, lane], state)
        for s in range(CHUNKS):
            enter(u, s, weight * state)
            if s < CHUNKS - 1:
                state = fade * state + chunk(1, c, s)
        gates(1, g, u)
        near(1, c)
        emit(c, u)

    def restore(into, g):
        cols = group(g)
        into[:, cols] = jnp.dot(back[...], gp[:, cols], preferred_element_type=F32).astype(BF16)

    halo_copy = pltpu.make_async_remote_copy(
        src_ref=halo_out, dst_ref=halo_in, send_sem=halo_sem.at[0], recv_sem=halo_sem.at[1],
        device_id=(lax.rem(me + 1, n_ctx), tp), device_id_type=MESH,
    )

    def twin_copy(g):
        return pltpu.make_async_remote_copy(
            src_ref=st_out.at[:, group(g)], dst_ref=twin_in.at[:, group(g)],
            send_sem=twin_send.at[g], recv_sem=twin_recv.at[g],
            device_id=(twin, tp), device_id_type=MESH,
        )

    def state_copy(g, src, dst):
        return pltpu.make_async_remote_copy(
            src_ref=both_out.at[:, group(g)], dst_ref=st_in.at[src, :, group(g)],
            send_sem=st_send.at[dst, g], recv_sem=st_recv.at[src, g],
            device_id=(dst * 2 + odd, tp), device_id_type=MESH,
        )

    def send_both(g):
        cols = group(g)
        twin_copy(g).wait_recv()
        other = twin_in[:, cols].astype(F32)
        own = own_end[:, cols]
        fade = decay_all[:, cols]
        total = jnp.where(odd == 1, fade * other + own, fade * own + other)
        both_out[:, cols] = total.astype(BF16)

        @pl.loop(pair + 1, n_ctx // 2)
        def _(dst):
            state_copy(g, pair, dst).start()

    rates_copy.wait()
    res_copy.wait()

    @pl.loop(0, tiles // 2)
    def _(k):
        responses(2 * k)
        responses(2 * k + 1)

    first_sent = jnp.where(odd == 1, FIRST[1], FIRST[0])
    second = jnp.where(odd == 1, SECOND[1], SECOND[0])
    tail_copy.wait()
    for j in range(3):
        halo_out[2 * j : 2 * j + 2, :] = tails[j].astype(F32)[TAIL - 2 :]
    halo_out[6:8, :] = jnp.zeros((2, channels), F32)
    taps_copy.wait()
    x_copy(0).wait()
    reorder(0, 0)

    @pl.loop(0, groups)
    def _(g):
        @pl.when(g < groups - 1)
        def _():
            x_copy(g + 1).wait()

        reorder(g, 1)
        last = ends(g, 1, ends(g, 0))
        reorder((g + 1) % groups, 0)
        ends(g, 3, ends(g, 2, last))

        @pl.when(g == 0)
        def _():
            pl.semaphore_wait(barrier, n_ctx + 1)

            @pl.when(me < n_ctx - 1)
            def _():
                halo_copy.start()

        @pl.when(g == HALO_GROUP)
        def _():
            @pl.when(me == 0)
            def _():
                halo_in[...] = jnp.zeros_like(halo_in)

            @pl.when(me > 0)
            def _():
                halo_copy.wait_recv()

        low = jnp.where(g == HALO_GROUP, 0, g)
        high = jnp.where(g < HALO_GROUP, low, g + 1)

        @pl.loop(low, high)
        def _(k):
            for u in range(UNITS):
                finish(k, u)
            twin_copy(k).start()

    @pl.loop(0, groups)
    def _(g):
        for u in range(UNITS):
            ahead(g, u)

        low = jnp.where(g == second, groups - 1, 0)
        high = jnp.where(g == second, groups, jnp.where(g == first_sent, groups - 1, 0))

        @pl.loop(low, high)
        def _(k):
            send_both(k)


    @pl.loop(0, groups)
    def _(g):
        cols = group(g)
        carry[:, cols] = jnp.zeros((modes, gwidth), F32)

        @pl.loop(0, pair)
        def _(src):
            fade = decay_all[:, cols] * decay_all[:, cols]
            state_copy(g, src, pair).wait_recv()
            carry[:, cols] = fade * carry[:, cols] + st_in[src, :, cols].astype(F32)

        @pl.when(odd == 1)
        def _():
            carry[:, cols] = decay_all[:, cols] * carry[:, cols] + twin_in[:, cols].astype(F32)

        for u in range(UNITS):
            carried_tile(g, u)
        restore(ga, g)

    w_copy.wait()

    def to_sibling(n, out, into, send, recv):
        return pltpu.make_async_remote_copy(
            src_ref=out.at[n], dst_ref=into.at[n], send_sem=send.at[n], recv_sem=recv.at[n],
            device_id=(me, sibling), device_id_type=MESH,
        )

    def pair_copy(n):
        return to_sibling(n, pair_out, pair_in, pair_send, pair_recv)

    def own_copy(n):
        return to_sibling(n, own_out, own_in, own_send, own_recv)

    def far_copy(n):
        return pltpu.make_async_remote_copy(
            src_ref=far_out.at[n], dst_ref=far_in.at[n],
            send_sem=far_send.at[n], recv_sem=far_recv.at[n],
            device_id=(me, opposite), device_id_type=MESH,
        )

    mine = pl.ds(pl.multiple_of(core * share, share), share)
    theirs = pl.ds(pl.multiple_of((1 - core) * share, share), share)

    def forward(n):
        pair_copy(n).wait_recv()
        far_out[n] = (keep[n] + pair_in[n].astype(F32)).astype(BF16)
        far_copy(n).start()

    def columns(n):
        return pl.ds(pl.multiple_of(n * WIDTH, WIDTH), WIDTH)

    @pl.loop(0, n_out)
    def _(n):
        pt[...] = jnp.dot(ga[...], wv[:, columns(n)], preferred_element_type=F32)
        pair_out[n] = pt[theirs, :].astype(BF16)
        pair_copy(n).start()
        keep[n] = pt[mine, :]

        @pl.when(n >= LAG)
        def _():
            forward(n - LAG)

    @pl.loop(n_out - LAG, n_out)
    def _(n):
        forward(n)

    @pl.loop(0, groups)
    def _(g):
        for u in range(UNITS):
            own_tile(g, u)
        restore(gb, g)

    @pl.loop(0, n_out)
    def _(n):
        pt[...] = jnp.dot(gb[...], wv[:, columns(n)], preferred_element_type=F32)
        own_out[n] = pt[theirs, :].astype(BF16)
        own_copy(n).start()
        kept[n] = pt[mine, :]

    @pl.loop(0, n_out)
    def _(n):
        own_copy(n).wait_recv()
        far_copy(n).wait_recv()
        total = kept[n] + own_in[n].astype(F32) + far_in[n].astype(F32)
        out_ref[:, columns(n)] = total.astype(BF16)

    @pl.loop(0, n_out)
    def _(n):
        pair_copy(n).wait_send()
        own_copy(n).wait_send()
        far_copy(n).wait_send()

    @pl.loop(0, groups)
    def _(g):
        twin_copy(g).wait_send()

        @pl.loop(pair + 1, n_ctx // 2)
        def _(dst):
            state_copy(g, pair, dst).wait_send()

    @pl.when(me < n_ctx - 1)
    def _():
        halo_copy.wait_send()


def per_device(n_ctx, projections, short_filter, decay_rates, residues, out_weight):
    x = jnp.transpose(projections, (1, 0, 2))
    _, toks, channels = x.shape
    modes = decay_rates.shape[0]
    dout = out_weight.shape[1]
    tiles = channels // LANES
    groups = tiles // UNITS
    n_out = dout // WIDTH
    share = toks // 4
    half = toks // 2
    step = half // CHUNKS
    rows = half + 2 * CHUNKS
    dma = pltpu.SemaphoreType.DMA
    hbm = pl.BlockSpec(memory_space=pltpu.HBM)
    operands = [
        pltpu.with_memory_space_constraint(a, pltpu.HBM)
        for a in (x, short_filter, decay_rates, residues, out_weight)
    ]
    return pl.pallas_call(
        functools.partial(kernel, n_ctx),
        out_shape=jax.ShapeDtypeStruct((share, dout), BF16),
        in_specs=[hbm] * 5,
        out_specs=pl.BlockSpec(memory_space=pltpu.VMEM),
        scratch_shapes=[
            pltpu.VMEM((3, toks, channels), BF16),
            pltpu.VMEM((3, TAIL, channels), BF16),
            pltpu.VMEM(short_filter.shape, F32),
            pltpu.VMEM((modes, channels), F32),
            pltpu.VMEM((modes, channels), F32),
            pltpu.VMEM((2 * rows, toks), BF16),
            pltpu.VMEM((half, half), BF16),
            pltpu.VMEM((3, 2, tiles // 2, rows, LANES), F32),
            pltpu.VMEM((3, 2, tiles // 2, rows, LANES), F32),
            pltpu.VMEM((2, tiles, half, LANES), F32),
            pltpu.VMEM((tiles, half, LANES), F32),
            pltpu.VMEM((tiles, half, LANES), F32),
            pltpu.VMEM((half, channels), BF16),
            pltpu.VMEM((half, channels), BF16),
            pltpu.VMEM((half, channels), BF16),
            pltpu.VMEM((channels, dout), BF16),
            pltpu.VMEM((half, WIDTH), F32),
            pltpu.VMEM((2, tiles, CHUNKS * (modes + 1), LANES), F32),
            pltpu.VMEM((tiles, CHUNKS, modes, LANES), F32),
            pltpu.VMEM((tiles, CHUNKS, modes, LANES), F32),
            pltpu.VMEM((UNITS, modes * (CHUNKS + 1), LANES), F32),
            pltpu.VMEM((tiles, step, LANES), F32),
            pltpu.VMEM((8, channels), F32),
            pltpu.VMEM((8, channels), F32),
            pltpu.VMEM((modes, channels), BF16),
            pltpu.VMEM((modes, channels), BF16),
            pltpu.VMEM((modes, channels), BF16),
            pltpu.VMEM((n_ctx // 2, modes, channels), BF16),
            pltpu.VMEM((modes, channels), F32),
            pltpu.VMEM((modes, channels), F32),
            pltpu.VMEM((modes, channels), F32),
            pltpu.VMEM((modes, channels), F32),
            pltpu.VMEM((n_out, share, WIDTH), F32),
            pltpu.VMEM((n_out, share, WIDTH), F32),
            pltpu.VMEM((n_out, share, WIDTH), BF16),
            pltpu.VMEM((n_out, share, WIDTH), BF16),
            pltpu.VMEM((n_out, share, WIDTH), BF16),
            pltpu.VMEM((n_out, share, WIDTH), BF16),
            pltpu.VMEM((n_out, share, WIDTH), BF16),
            pltpu.VMEM((n_out, share, WIDTH), BF16),
            dma((groups,)), dma((4,)), dma, dma((2,)),
            dma((groups,)), dma((groups,)),
            dma((n_ctx // 2, groups)), dma((n_ctx // 2, groups)),
            dma((n_out,)), dma((n_out,)), dma((n_out,)), dma((n_out,)),
            dma((n_out,)), dma((n_out,)),
        ],
        compiler_params=pltpu.CompilerParams(
            collective_id=0, has_side_effects=True, vmem_limit_bytes=48 * 2**20
        ),
    )(*operands)


def solution(mesh):
    placed = (
        P("ctx", None, "tp"),
        P(None, None, "tp"),
        P(None, "tp"),
        P(None, "tp"),
        P("tp", None),
    )
    return jax.shard_map(
        functools.partial(per_device, mesh.shape["ctx"]),
        mesh=mesh, in_specs=placed, out_specs=P(("ctx", "tp"), None), check_vma=False,
    )
```

```python
import functools

import jax
import jax.numpy as jnp
from jax import lax
from jax.experimental import pallas as pl
from jax.experimental.pallas import tpu as pltpu
from jax.sharding import PartitionSpec as P

LANES = 128
CHUNKS = 8
UNITS = 4
HALO_GROUP = 3
MXU = 256
WIDTH = 512
FIRST = (2, 2)
SECOND = (3, 3)
LAG = 2
TAIL = 16
MESH = pl.DeviceIdType.MESH
F32 = jnp.float32
BF16 = jnp.bfloat16


def summed(terms):
    while terms.shape[0] % 2 == 0:
        middle = terms.shape[0] // 2
        terms = terms[:middle] + terms[middle:]
    return jnp.sum(terms, axis=0)


def kernel(
    n_ctx, x_hbm, taps_hbm, rates_hbm, res_hbm, w_hbm, out_ref,
    xb, tails, taps_ref, rates_ref, res_ref, order, back, xs_even, xs_odd, pf, qf, yl, gp, ga, gb, wv, pt, raw, base, fades, entry, hb,
    halo_out, halo_in, st_out, twin_in, both_out, st_in,
    own_end, decay_all, carry, first, keep, kept, pair_out, pair_in, own_out, own_in, far_out, far_in,
    x_sem, in_sem, w_sem, halo_sem, twin_send, twin_recv, st_send, st_recv,
    pair_send, pair_recv, own_send, own_recv, far_send, far_recv,
):
    me = lax.axis_index("ctx")
    tp = lax.axis_index("tp")
    pair, odd = me // 2, me % 2
    twin = pair * 2 + (1 - odd)
    chip, core = tp // 2, tp % 2
    sibling = chip * 2 + (1 - core)
    opposite = (1 - chip) * 2 + core
    toks, channels = xb.shape[1], xb.shape[2]
    modes = rates_ref.shape[0]
    half = toks // 2
    step = half // CHUNKS
    rows = half + 2 * CHUNKS
    gwidth = UNITS * LANES
    tiles = channels // LANES
    groups = channels // gwidth
    per_block = MXU // LANES
    n_out = w_hbm.shape[1] // WIDTH
    share = toks // 4
    early = 1 - chip

    def group(g):
        return pl.ds(pl.multiple_of(g * gwidth, gwidth), gwidth)

    def x_copy(g):
        return pltpu.make_async_copy(x_hbm.at[:, :, group(g)], xb.at[:, :, group(g)], x_sem.at[g])

    tail_copy = pltpu.make_async_copy(x_hbm.at[:, toks - TAIL :, :], tails, in_sem.at[0])
    rates_copy = pltpu.make_async_copy(rates_hbm, rates_ref, in_sem.at[1])
    taps_copy = pltpu.make_async_copy(taps_hbm, taps_ref, in_sem.at[2])
    res_copy = pltpu.make_async_copy(res_hbm, res_ref, in_sem.at[3])
    w_copy = pltpu.make_async_copy(w_hbm, wv, w_sem)

    rates_copy.start()
    res_copy.start()
    x_copy(0).start()
    taps_copy.start()
    tail_copy.start()

    @pl.loop(1, groups)
    def _(g):
        x_copy(g).start()

    w_copy.start()

    barrier = pltpu.get_barrier_semaphore()

    @pl.loop(1, n_ctx)
    def _(k):
        pl.semaphore_signal(
            barrier, inc=1, device_id=(lax.rem(me + k, n_ctx), tp), device_id_type=MESH
        )

    for other in (sibling, opposite):
        pl.semaphore_signal(barrier, inc=1, device_id=(me, other), device_id_type=MESH)

    for b in range(2):
        row = lax.broadcasted_iota(jnp.int32, (rows, toks), 0)
        token = lax.broadcasted_iota(jnp.int32, (rows, toks), 1)
        start = early * half if b == 0 else chip * half
        wanted = start + (row % CHUNKS) * step + row // CHUNKS - 2
        order[b * rows : (b + 1) * rows, :] = jnp.where(token == wanted, 1.0, 0.0).astype(BF16)
    token = lax.broadcasted_iota(jnp.int32, (half, half), 0)
    row = lax.broadcasted_iota(jnp.int32, (half, half), 1)
    back[...] = jnp.where(token == (row % CHUNKS) * step + row // CHUNKS, 1.0, 0.0).astype(BF16)

    place = lax.broadcasted_iota(jnp.int32, (1, CHUNKS, LANES), 1)
    late_block = jnp.where(chip == 0, 1.0, 0.0).astype(F32)

    def spread(values):
        return jnp.broadcast_to(values[:, None, :], (values.shape[0], CHUNKS, LANES))

    def lanes(c):
        return pl.ds(pl.multiple_of(c * LANES, LANES), LANES)

    def collapse(terms):
        spot = place[0]
        out = []
        for f in range(0, len(terms), CHUNKS):
            v = terms[f : f + CHUNKS]
            low = spot < 4
            y = [
                jnp.where(low, v[n], v[n + 4]) + pltpu.roll(jnp.where(low, v[n + 4], v[n]), 4, 0)
                for n in range(4)
            ]
            low = spot % 4 < 2
            z = [
                jnp.where(low, y[n] + pltpu.roll(y[n], 6, 0), y[n + 2] + pltpu.roll(y[n + 2], 2, 0))
                for n in range(2)
            ]
            low = spot % 2 == 0
            out.append(jnp.where(low, z[0] + pltpu.roll(z[0], 7, 0), z[1] + pltpu.roll(z[1], 1, 0)))
        return jnp.concatenate(out, axis=0)

    def ordered(g, u):
        return (xs_even, xs_odd)[u // per_block], g * per_block + u % per_block

    def reorder(g, which):
        cols = pl.ds(pl.multiple_of(g * gwidth + which * MXU, MXU), MXU)
        for j in range(3):
            moved = jnp.dot(order[...], xb[j, :, cols], preferred_element_type=F32)
            for b in range(2):
                for u in range(which * per_block, (which + 1) * per_block):
                    xs, at = ordered(g, u)
                    left = u % per_block * LANES
                    xs[j, b, at] = moved[b * rows : (b + 1) * rows, left : left + LANES]

    def feature(j, b, g, u, low, high):
        lane = lanes(g * UNITS + u)
        xs, where = ordered(g, u)
        total = None
        for i in range(3):
            at = (2 - i) * CHUNKS
            term = taps_ref[i, j : j + 1, lane] * xs[j, b, where, at + low : at + high, :]
            total = term if total is None else total + term
        return total

    def add_halo(j, g, u):
        lane = lanes(g * UNITS + u)
        xs, where = ordered(g, u)
        xs[j, early, where, 0:1, :] = halo_in[2 * j : 2 * j + 1, lane]
        xs[j, early, where, CHUNKS : CHUNKS + 1, :] = halo_in[2 * j + 1 : 2 * j + 2, lane]

    def chunk(b, c, s):
        return raw[b, c, s * (modes + 1) : s * (modes + 1) + modes, :]

    def ends(g, u, last=None):
        c = g * UNITS + u
        decay = jnp.exp(-spread(rates_ref[:, lanes(c)]))
        for b in range(2):
            product = feature(1, b, g, u, 0, half) * feature(2, b, g, u, 0, half)
            pf[b, c] = product
            opening = product[:CHUNKS]
            if last is not None:
                opening = opening + 0.0 * last
            state = jnp.broadcast_to(opening[None], (modes, CHUNKS, LANES))
            for i in range(1, step):
                state = decay * state + product[None, i * CHUNKS : (i + 1) * CHUNKS]
            for n in range(modes):
                raw[b, c, pl.ds(n, CHUNKS, stride=modes + 1), :] = state[n]
            last = state[modes - 1]
        return last

    def finish(g, u):
        c = g * UNITS + u
        lane = lanes(c)
        rates = rates_ref[:, lane]
        two = 2 * CHUNKS
        for j in (1, 2):
            add_halo(j, g, u)
        product = feature(1, early, g, u, 0, two) * feature(2, early, g, u, 0, two)
        change = product - pf[early, c, :two, :]
        pf[early, c, :two, :] = product
        grown = jnp.exp(-rates) * change[:1] + change[CHUNKS : CHUNKS + 1]
        end = chunk(early, c, 0) + jnp.exp(-rates * float(step - 2)) * grown
        raw[early, c, 0:modes, :] = end
        fade = jnp.exp(-rates * float(step))
        for s in range(1, CHUNKS):
            end = fade * end + chunk(early, c, s)
        first[:, lane] = end
        for s in range(CHUNKS):
            end = fade * end + chunk(chip, c, s)
        own_end[:, lane] = end
        st_out[:, lane] = end.astype(BF16)

    def near(b, c):
        for i in range(step):
            total = None
            for k in range(i + 1):
                at = (i - k) * CHUNKS
                term = hb[c, k : k + 1, :] * pf[b, c, at : at + CHUNKS, :]
                total = term if total is None else total + term
            yl[c, i * CHUNKS : (i + 1) * CHUNKS, :] = total

    def responses(c):
        lane = lanes(c)
        rates = rates_ref[:, lane]
        decay = jnp.exp(-rates)
        now = res_ref[:, lane] * jnp.sqrt(2.0 * rates)
        terms = []
        for i in range(step):
            terms.append(summed(now.reshape(modes // CHUNKS, CHUNKS, LANES)))
            now = now * decay
        hb[c] = collapse(terms)
        decay_all[:, lane] = jnp.exp(-rates * float(toks))

    def gates(b, g, u):
        if b == 0:
            add_halo(0, g, u)
        qf[g * UNITS + u] = feature(0, b, g, u, 0, half)

    def weights(lane, rates):
        return res_ref[:, lane] * jnp.sqrt(2.0 * rates) * jnp.exp(-rates)

    def ahead(g, u):
        c = g * UNITS + u
        lane = lanes(c)
        rates = rates_ref[:, lane]
        weight = weights(lane, rates)
        fade = jnp.exp(-rates * float(step))
        state = first[:, lane] * late_block
        reach = weight * jnp.exp(-rates * (float(half) * late_block))
        for s in range(CHUNKS):
            base[c, s] = weight * state
            fades[c, s] = reach
            if s < CHUNKS - 1:
                state = fade * state + chunk(0, c, s)
                reach = fade * reach
        gates(0, g, u)
        near(0, c)

    def enter(u, s, state):
        entry[u, pl.ds(s, modes, stride=CHUNKS + 1), :] = state

    def emit(c, u):
        lane = lanes(c)
        decay = spread(jnp.exp(-rates_ref[:, lane]))
        state = [entry[u, n * (CHUNKS + 1) : n * (CHUNKS + 1) + CHUNKS, :] for n in range(modes)]
        for i in range(0, step, 2):
            parts = []
            for k in (i, i + 1):
                at = slice(k * CHUNKS, (k + 1) * CHUNKS)
                terms = state
                while len(terms) > 1:
                    middle = len(terms) // 2
                    terms = [terms[n] + terms[n + middle] for n in range(middle)]
                parts.append(qf[c, at, :] * (yl[c, at, :] + terms[0]))
                state = [decay[n] * state[n] for n in range(modes)]
            gp[i * CHUNKS : (i + 2) * CHUNKS, lane] = jnp.concatenate(parts, axis=0).astype(BF16)

    def carried_tile(g, u):
        c = g * UNITS + u
        into = carry[:, lanes(c)]
        for s in range(CHUNKS):
            enter(u, s, base[c, s] + fades[c, s] * into)
        emit(c, u)

    def own_tile(g, u):
        c = g * UNITS + u
        lane = lanes(c)
        rates = rates_ref[:, lane]
        weight = weights(lane, rates)
        fade = jnp.exp(-rates * float(step))
        state = carry[:, lane]
        state = jnp.where(chip == 1, jnp.exp(-rates * float(half)) * state + first[:, lane], state)
        for s in range(CHUNKS):
            enter(u, s, weight * state)
            if s < CHUNKS - 1:
                state = fade * state + chunk(1, c, s)
        gates(1, g, u)
        near(1, c)
        emit(c, u)

    def restore(into, g):
        cols = group(g)
        into[:, cols] = jnp.dot(back[...], gp[:, cols], preferred_element_type=F32).astype(BF16)

    halo_copy = pltpu.make_async_remote_copy(
        src_ref=halo_out, dst_ref=halo_in, send_sem=halo_sem.at[0], recv_sem=halo_sem.at[1],
        device_id=(lax.rem(me + 1, n_ctx), tp), device_id_type=MESH,
    )

    def twin_copy(g):
        return pltpu.make_async_remote_copy(
            src_ref=st_out.at[:, group(g)], dst_ref=twin_in.at[:, group(g)],
            send_sem=twin_send.at[g], recv_sem=twin_recv.at[g],
            device_id=(twin, tp), device_id_type=MESH,
        )

    def state_copy(g, src, dst):
        return pltpu.make_async_remote_copy(
            src_ref=both_out.at[:, group(g)], dst_ref=st_in.at[src, :, group(g)],
            send_sem=st_send.at[dst, g], recv_sem=st_recv.at[src, g],
            device_id=(dst * 2 + odd, tp), device_id_type=MESH,
        )

    def send_both(g):
        cols = group(g)
        twin_copy(g).wait_recv()
        other = twin_in[:, cols].astype(F32)
        own = own_end[:, cols]
        fade = decay_all[:, cols]
        total = jnp.where(odd == 1, fade * other + own, fade * own + other)
        both_out[:, cols] = total.astype(BF16)

        @pl.loop(pair + 1, n_ctx // 2)
        def _(dst):
            state_copy(g, pair, dst).start()

    rates_copy.wait()
    res_copy.wait()

    @pl.loop(0, tiles // 2)
    def _(k):
        responses(2 * k)
        responses(2 * k + 1)

    first_sent = jnp.where(odd == 1, FIRST[1], FIRST[0])
    second = jnp.where(odd == 1, SECOND[1], SECOND[0])
    tail_copy.wait()
    for j in range(3):
        halo_out[2 * j : 2 * j + 2, :] = tails[j].astype(F32)[TAIL - 2 :]
    halo_out[6:8, :] = jnp.zeros((2, channels), F32)
    taps_copy.wait()
    x_copy(0).wait()
    reorder(0, 0)

    @pl.loop(0, groups)
    def _(g):
        @pl.when(g < groups - 1)
        def _():
            x_copy(g + 1).wait()

        reorder(g, 1)
        last = ends(g, 1, ends(g, 0))
        reorder((g + 1) % groups, 0)
        ends(g, 3, ends(g, 2, last))

        @pl.when(g == 0)
        def _():
            pl.semaphore_wait(barrier, n_ctx + 1)

            @pl.when(me < n_ctx - 1)
            def _():
                halo_copy.start()

        @pl.when(g == HALO_GROUP)
        def _():
            @pl.when(me == 0)
            def _():
                halo_in[...] = jnp.zeros_like(halo_in)

            @pl.when(me > 0)
            def _():
                halo_copy.wait_recv()

        low = jnp.where(g == HALO_GROUP, 0, g)
        high = jnp.where(g < HALO_GROUP, low, g + 1)

        @pl.loop(low, high)
        def _(k):
            for u in range(UNITS):
                finish(k, u)
            twin_copy(k).start()

    @pl.loop(0, groups)
    def _(g):
        for u in range(UNITS):
            ahead(g, u)

        low = jnp.where(g == second, groups - 1, 0)
        high = jnp.where(g == second, groups, jnp.where(g == first_sent, groups - 1, 0))

        @pl.loop(low, high)
        def _(k):
            send_both(k)


    @pl.loop(0, groups)
    def _(g):
        cols = group(g)
        carry[:, cols] = jnp.zeros((modes, gwidth), F32)

        @pl.loop(0, pair)
        def _(src):
            fade = decay_all[:, cols] * decay_all[:, cols]
            state_copy(g, src, pair).wait_recv()
            carry[:, cols] = fade * carry[:, cols] + st_in[src, :, cols].astype(F32)

        @pl.when(odd == 1)
        def _():
            carry[:, cols] = decay_all[:, cols] * carry[:, cols] + twin_in[:, cols].astype(F32)

        for u in range(UNITS):
            carried_tile(g, u)
        restore(ga, g)

    w_copy.wait()

    def to_sibling(n, out, into, send, recv):
        return pltpu.make_async_remote_copy(
            src_ref=out.at[n], dst_ref=into.at[n], send_sem=send.at[n], recv_sem=recv.at[n],
            device_id=(me, sibling), device_id_type=MESH,
        )

    def pair_copy(n):
        return to_sibling(n, pair_out, pair_in, pair_send, pair_recv)

    def own_copy(n):
        return to_sibling(n, own_out, own_in, own_send, own_recv)

    def far_copy(n):
        return pltpu.make_async_remote_copy(
            src_ref=far_out.at[n], dst_ref=far_in.at[n],
            send_sem=far_send.at[n], recv_sem=far_recv.at[n],
            device_id=(me, opposite), device_id_type=MESH,
        )

    mine = pl.ds(pl.multiple_of(core * share, share), share)
    theirs = pl.ds(pl.multiple_of((1 - core) * share, share), share)

    def forward(n):
        pair_copy(n).wait_recv()
        far_out[n] = (keep[n] + pair_in[n].astype(F32)).astype(BF16)
        far_copy(n).start()

    def columns(n):
        return pl.ds(pl.multiple_of(n * WIDTH, WIDTH), WIDTH)

    @pl.loop(0, n_out)
    def _(n):
        pt[...] = jnp.dot(ga[...], wv[:, columns(n)], preferred_element_type=F32)
        pair_out[n] = pt[theirs, :].astype(BF16)
        pair_copy(n).start()
        keep[n] = pt[mine, :]

        @pl.when(n >= LAG)
        def _():
            forward(n - LAG)

    @pl.loop(n_out - LAG, n_out)
    def _(n):
        forward(n)

    @pl.loop(0, groups)
    def _(g):
        for u in range(UNITS):
            own_tile(g, u)
        restore(gb, g)

    @pl.loop(0, n_out)
    def _(n):
        pt[...] = jnp.dot(gb[...], wv[:, columns(n)], preferred_element_type=F32)
        own_out[n] = pt[theirs, :].astype(BF16)
        own_copy(n).start()
        kept[n] = pt[mine, :]

    @pl.loop(0, n_out)
    def _(n):
        pair_copy(n).wait_send()
        own_copy(n).wait_send()

    @pl.loop(0, groups)
    def _(g):
        twin_copy(g).wait_send()

        @pl.loop(pair + 1, n_ctx // 2)
        def _(dst):
            state_copy(g, pair, dst).wait_send()

    @pl.when(me < n_ctx - 1)
    def _():
        halo_copy.wait_send()

    @pl.loop(0, n_out)
    def _(n):
        own_copy(n).wait_recv()
        far_copy(n).wait_recv()
        total = kept[n] + own_in[n].astype(F32) + far_in[n].astype(F32)
        out_ref[:, columns(n)] = total.astype(BF16)

    @pl.loop(0, n_out)
    def _(n):
        far_copy(n).wait_send()


def per_device(n_ctx, projections, short_filter, decay_rates, residues, out_weight):
    x = jnp.transpose(projections, (1, 0, 2))
    _, toks, channels = x.shape
    modes = decay_rates.shape[0]
    dout = out_weight.shape[1]
    tiles = channels // LANES
    groups = tiles // UNITS
    n_out = dout // WIDTH
    share = toks // 4
    half = toks // 2
    step = half // CHUNKS
    rows = half + 2 * CHUNKS
    dma = pltpu.SemaphoreType.DMA
    hbm = pl.BlockSpec(memory_space=pltpu.HBM)
    operands = [
        pltpu.with_memory_space_constraint(a, pltpu.HBM)
        for a in (x, short_filter, decay_rates, residues, out_weight)
    ]
    return pl.pallas_call(
        functools.partial(kernel, n_ctx),
        out_shape=jax.ShapeDtypeStruct((share, dout), BF16),
        in_specs=[hbm] * 5,
        out_specs=pl.BlockSpec(memory_space=pltpu.VMEM),
        scratch_shapes=[
            pltpu.VMEM((3, toks, channels), BF16),
            pltpu.VMEM((3, TAIL, channels), BF16),
            pltpu.VMEM(short_filter.shape, F32),
            pltpu.VMEM((modes, channels), F32),
            pltpu.VMEM((modes, channels), F32),
            pltpu.VMEM((2 * rows, toks), BF16),
            pltpu.VMEM((half, half), BF16),
            pltpu.VMEM((3, 2, tiles // 2, rows, LANES), F32),
            pltpu.VMEM((3, 2, tiles // 2, rows, LANES), F32),
            pltpu.VMEM((2, tiles, half, LANES), F32),
            pltpu.VMEM((tiles, half, LANES), F32),
            pltpu.VMEM((tiles, half, LANES), F32),
            pltpu.VMEM((half, channels), BF16),
            pltpu.VMEM((half, channels), BF16),
            pltpu.VMEM((half, channels), BF16),
            pltpu.VMEM((channels, dout), BF16),
            pltpu.VMEM((half, WIDTH), F32),
            pltpu.VMEM((2, tiles, CHUNKS * (modes + 1), LANES), F32),
            pltpu.VMEM((tiles, CHUNKS, modes, LANES), F32),
            pltpu.VMEM((tiles, CHUNKS, modes, LANES), F32),
            pltpu.VMEM((UNITS, modes * (CHUNKS + 1), LANES), F32),
            pltpu.VMEM((tiles, step, LANES), F32),
            pltpu.VMEM((8, channels), F32),
            pltpu.VMEM((8, channels), F32),
            pltpu.VMEM((modes, channels), BF16),
            pltpu.VMEM((modes, channels), BF16),
            pltpu.VMEM((modes, channels), BF16),
            pltpu.VMEM((n_ctx // 2, modes, channels), BF16),
            pltpu.VMEM((modes, channels), F32),
            pltpu.VMEM((modes, channels), F32),
            pltpu.VMEM((modes, channels), F32),
            pltpu.VMEM((modes, channels), F32),
            pltpu.VMEM((n_out, share, WIDTH), F32),
            pltpu.VMEM((n_out, share, WIDTH), F32),
            pltpu.VMEM((n_out, share, WIDTH), BF16),
            pltpu.VMEM((n_out, share, WIDTH), BF16),
            pltpu.VMEM((n_out, share, WIDTH), BF16),
            pltpu.VMEM((n_out, share, WIDTH), BF16),
            pltpu.VMEM((n_out, share, WIDTH), BF16),
            pltpu.VMEM((n_out, share, WIDTH), BF16),
            dma((groups,)), dma((4,)), dma, dma((2,)),
            dma((groups,)), dma((groups,)),
            dma((n_ctx // 2, groups)), dma((n_ctx // 2, groups)),
            dma((n_out,)), dma((n_out,)), dma((n_out,)), dma((n_out,)),
            dma((n_out,)), dma((n_out,)),
        ],
        compiler_params=pltpu.CompilerParams(
            collective_id=0, has_side_effects=True, vmem_limit_bytes=48 * 2**20
        ),
    )(*operands)


def solution(mesh):
    placed = (
        P("ctx", None, "tp"),
        P(None, None, "tp"),
        P(None, "tp"),
        P(None, "tp"),
        P("tp", None),
    )
    return jax.shard_map(
        functools.partial(per_device, mesh.shape["ctx"]),
        mesh=mesh, in_specs=placed, out_specs=P(("ctx", "tp"), None), check_vma=False,
    )
```
